256 devices in a mesh: seq: 4 (over x), head: 64 (over y, z, core).
Axes of the slice: x: 4, y: 4, z: 8, core: 2. Of those that a mesh axis runs over, the one named last changes fastest.
Arguments:
- queries: bfloat16 [4096, 64, 128], P(('seq', 'head')), may hold values from -160 to 160
- keys: bfloat16 [4096, 64, 128], P(('seq', 'head')), may hold values from -8 to 8
- b_proj: bfloat16 [4096, 64, 128], P(('seq', 'head')), may hold values from -6 to 6
- c_proj: bfloat16 [4096, 64, 128], P(('seq', 'head')), may hold values from -6 to 6
- step_size: bfloat16 [4096, 64], P(('seq', 'head')), may hold values from 0 to 110
- rate_level: int32 [64], P('head'), may hold values from 0 to 15
Outputs:
- grad_b: float32 [4096, 64, 128], P(('seq', 'head'))
- grad_c: float32 [4096, 64, 128], P(('seq', 'head'))
- grad_step: float32 [4096, 64], P(('seq', 'head'))
- loss: float32 [], replicated
The draws below stay inside these ranges and needn't reach their ends.
All inputs are finite; a program needn't handle non-finite values.
Results may differ from the reference program's by a relative error of at most 0.00098.
Values may be sent and summed in bfloat16 or wider, within the bound.
No kernel may reach another device: no remote copies, remote signals or barrier semaphores. Data moves between devices by JAX's collectives and lax.ppermute only.
A program may use at most 128 MiB of HBM per device.

```python
import math
import jax
import jax.numpy as jnp
from jax import lax

HEAD_DIM = 128
STATE = 128
TEXT_SPAN = 4096
PAIRS = 64


def shared_keys(key):
    return jnp.clip(jax.random.normal(key, (TEXT_SPAN, PAIRS, HEAD_DIM), jnp.float32), -6.0, 6.0)


def shared_levels(key):
    order = jax.random.permutation(jax.random.fold_in(key, 2), PAIRS)
    return (order * 16 // PAIRS).astype(jnp.int32)


def draw_keys(key, part):
    floor_offset = shared_keys(key)
    return floor_offset.astype(jnp.bfloat16)


def draw_queries(key, part):
    floor_offset = shared_keys(key)
    key = jax.random.fold_in(key, 5)
    own = jnp.clip(jax.random.normal(key, floor_offset.shape, jnp.float32), -6.0, 6.0)
    return own.astype(jnp.bfloat16)


def draw_rate_level(key, part):
    return shared_levels(key)


def draw_step_size(key, part):
    level = shared_levels(key)
    key = jax.random.fold_in(key, 4)
    parts_keys = jax.random.split(key, 4)
    low = 2e-05
    high = 0.04
    floor_offset = jnp.exp(jax.random.uniform(parts_keys[0], (1, PAIRS), jnp.float32, math.log(low), math.log(high)))
    random_jitter = jax.random.uniform(parts_keys[1], (TEXT_SPAN, PAIRS), jnp.float32, 0.5, 1.5)
    jump_indices = jax.random.randint(parts_keys[2], (3, PAIRS), 0, TEXT_SPAN)
    sudden_jump = jnp.any(jnp.arange(TEXT_SPAN)[:, None, None] == jump_indices[None], axis=1)
    jitter_scale = jax.random.uniform(parts_keys[3], (TEXT_SPAN, PAIRS), jnp.float32, 0.22, 0.5)
    natural_log_decay = floor_offset * random_jitter + jnp.where(sudden_jump, jitter_scale, 0.0)
    return (natural_log_decay * jnp.exp2(0.5 * level.astype(jnp.float32))[None, :]).astype(jnp.bfloat16)


def block_levels(rng, shape, pieces, low, high):
    def one(dim, shards_of):
        heights = jax.random.uniform(jax.random.fold_in(jax.random.fold_in(rng, 6), dim), (shards_of,), jnp.float32, low / len(pieces), high / len(pieces))
        return jnp.repeat(jnp.exp(heights), shape[dim] // shards_of).reshape((-1,) + (1,) * (len(shape) - dim - 1))

    level = one(*pieces[0])
    for cut in pieces[1:]:
        level = level * one(*cut)
    return level


def normal_values(stream_key, extent, scale, limit, pieces=(), kind=jnp.bfloat16):
    factor_of = block_levels(stream_key, extent, pieces, -0.22, 0.18) if pieces else 1.0
    array = jax.random.normal(stream_key, extent, jnp.float32) * scale * factor_of
    return jnp.minimum(jnp.maximum(array, -limit), limit).astype(kind)


def setup_inputs(seed: int = 0) -> dict:
    streams_of = jax.random.split(jax.random.key(seed), 7)
    return {
        "queries": draw_queries(jax.random.fold_in(streams_of[6], 71), 0),
        "keys": draw_keys(jax.random.fold_in(streams_of[6], 71), 0),
        "b_proj": normal_values(streams_of[2], (TEXT_SPAN, PAIRS, STATE), 1.0, 6.0, ((0, 256),)),
        "c_proj": normal_values(streams_of[3], (TEXT_SPAN, PAIRS, STATE), 1.0, 6.0, ((0, 256),)),
        "step_size": draw_step_size(jax.random.fold_in(streams_of[6], 71), 0),
        "rate_level": draw_rate_level(jax.random.fold_in(streams_of[6], 71), 0),
    }


def reference(queries, keys, b_proj, c_proj, step_size, rate_level):
    rate = jnp.exp2(-0.5 * rate_level.astype(jnp.float32))
    log_decay = -rate[None, :] * step_size.astype(jnp.float32)
    sums = jnp.cumsum(log_decay, axis=0)
    beta = 2.0 / math.sqrt(STATE * TEXT_SPAN)
    places = jnp.arange(TEXT_SPAN, dtype=jnp.int32)
    causal = places[None, :] <= places[:, None]

    def one_pair(items):
        query, key_row, b_row, c_row, sum_row = items
        scores = jnp.dot(query, key_row.T, preferred_element_type=jnp.float32) / math.sqrt(HEAD_DIM)
        masked = jnp.where(causal, scores, -jnp.inf)
        top = lax.optimization_barrier(jnp.max(masked, axis=1, keepdims=True))
        raised = jnp.exp(masked - top)
        teacher = raised / lax.optimization_barrier(jnp.sum(raised, axis=1, keepdims=True))
        decay = jnp.exp(jnp.where(causal, sum_row[:, None] - sum_row[None, :], -jnp.inf))
        student = beta * jnp.dot(c_row, b_row.T, preferred_element_type=jnp.float32) * decay
        error = student - teacher
        sumsq = jnp.sum(error * error)
        held = (error * decay).astype(jnp.bfloat16)
        grad_c = jnp.dot(held, b_row, preferred_element_type=jnp.float32)
        grad_b = jnp.dot(held.T, c_row, preferred_element_type=jnp.float32)
        weight = error * student
        slope = lax.optimization_barrier(jnp.sum(weight, axis=1)) - lax.optimization_barrier(jnp.sum(weight, axis=0))
        return (grad_c, grad_b, slope, sumsq)
    grad_c, grad_b, slope, sumsq = lax.map(one_pair, (jnp.transpose(queries, (1, 0, 2)), jnp.transpose(keys, (1, 0, 2)), jnp.transpose(b_proj, (1, 0, 2)), jnp.transpose(c_proj, (1, 0, 2)), sums.T))
    norm = jnp.sqrt(sumsq + 1e-06)
    factor = TEXT_SPAN / norm
    tails = jnp.cumsum(slope[:, ::-1], axis=1)[:, ::-1]
    grad_b_out = jnp.transpose(grad_b, (1, 0, 2)) * (factor * beta)[None, :, None]
    grad_c_out = jnp.transpose(grad_c, (1, 0, 2)) * (factor * beta)[None, :, None]
    grad_step = tails.T * (-(rate * factor))[None, :]
    loss = jnp.mean(norm)
    return (grad_b_out, grad_c_out, grad_step, loss)
```

```python
import functools
import math

import jax
import jax.numpy as jnp
from jax import lax
from jax.experimental import pallas as pl
from jax.experimental.pallas import tpu as pltpu
from jax.sharding import PartitionSpec as P

F32 = jnp.float32
BF16 = jnp.bfloat16
F16 = jnp.float16
LOG2E = math.log2(math.e)
TILE = 256
LOWEST = -1e30
VMEM_BYTES = 56 * 1024 * 1024


def dot_nt(a, b):
    return lax.dot_general(a, b, (((1,), (1,)), ((), ())), preferred_element_type=F32)


def dot_nn(a, b):
    return lax.dot_general(a, b, (((1,), (0,)), ((), ())), preferred_element_type=F32)


def dot_full(a, b):
    return lax.dot_general(
        a, b, (((1,), (0,)), ((), ())),
        precision=lax.Precision.HIGHEST, preferred_element_type=F32,
    )


def fold_rows(x):
    rows, cols = x.shape
    x = jnp.sum(x.reshape(rows // 8, 8, cols), axis=0)
    out = x[:, :128]
    for at in range(128, cols, 128):
        out = out + x[:, at:at + 128]
    return out


def total_of(x):
    return jnp.sum(jnp.sum(x, axis=0, keepdims=True), axis=1, keepdims=True)


def exponent_of(x):
    top = jnp.max(jnp.max(jnp.abs(x), axis=0, keepdims=True), axis=1, keepdims=True)
    return jnp.floor(jnp.log2(jnp.maximum(top, 1e-30)))


def earlier_kernel(
    scale, beta, block_ref, qc_ref, kb0_ref, kb1_ref, kb2_ref, kb3_ref, vec_ref,
    part1_ref, part2_ref, part3_ref, gc_ref, top_ref, rinv_ref, small_ref,
    q_s, c_s, ct_s, k_s, b_s, max_s, sum_s, gbt_s, cols_s, sq_s,
):
    block = block_ref[0]
    rows, width = q_s.shape
    n = qc_ref.shape[1] // 2
    tiles = rows // TILE
    q_s[...] = qc_ref[:, 0:n, :].reshape(rows, width)
    c_s[...] = qc_ref[:, n:2 * n, :].reshape(rows, width)
    ct_s[...] = jnp.transpose(c_s[...].astype(F32)).astype(BF16)
    cols_s[...] = jnp.transpose(vec_ref[...])
    kbs = (kb0_ref, kb1_ref, kb2_ref, kb3_ref)
    parts = (None, part1_ref, part2_ref, part3_ref)
    max_s[...] = jnp.full(max_s.shape, LOWEST, F32)
    sum_s[...] = jnp.zeros(sum_s.shape, F32)
    gc_ref[...] = jnp.zeros(gc_ref.shape, F32)
    small_ref[...] = jnp.zeros(small_ref.shape, F32)
    sq_s[...] = jnp.zeros(sq_s.shape, F32)

    def stats(at, d, size, masked):
        ti = pl.ds(at, TILE)
        s = dot_nt(q_s[ti, :], k_s[d, 0:size, :])
        if masked:
            row = lax.broadcasted_iota(jnp.int32, s.shape, 0) + at
            col = lax.broadcasted_iota(jnp.int32, s.shape, 1)
            s = jnp.where(col <= row, s, LOWEST)
        old = max_s[ti, :]
        new = old
        for g in range(0, size, 128):
            new = jnp.maximum(new, s[:, g:g + 128])
        acc = sum_s[ti, :] * jnp.exp2((old - new) * scale)
        for g in range(0, size, 128):
            acc = acc + jnp.exp2((s[:, g:g + 128] - new) * scale)
        max_s[ti, :] = new
        sum_s[ti, :] = acc

    for d in range(4):
        @pl.when(block >= d)
        def _(d=d):
            k_s[d, :, :] = kbs[d][:, 0:n, :].reshape(rows, width)
            b_s[d, :, :] = kbs[d][:, n:2 * n, :].reshape(rows, width)
            if d == 0:
                for it in range(tiles):
                    stats(it * TILE, 0, (it + 1) * TILE, True)
            else:
                @pl.loop(0, tiles)
                def _(it):
                    stats(pl.multiple_of(it * TILE, TILE), d, rows, False)

    top = jnp.max(max_s[...], axis=1, keepdims=True)
    total = jnp.sum(sum_s[...] * jnp.exp2((max_s[...] - top) * scale), axis=1, keepdims=True)
    top_ref[...] = jnp.broadcast_to(top, top_ref.shape)
    rinv_ref[...] = jnp.broadcast_to(1.0 / total, rinv_ref.shape)

    for d in range(1, 4):
        @pl.when(block >= d)
        def _(d=d):
            gbt_s[...] = jnp.zeros(gbt_s.shape, F32)

            @pl.loop(0, tiles)
            def _(it):
                ti = pl.ds(pl.multiple_of(it * TILE, TILE), TILE)
                q, c, ct = q_s[ti, :], c_s[ti, :], ct_s[:, ti]
                top_i = top_ref[ti, 0:1]
                rinv_i = rinv_ref[ti, 0:1]
                u_i = cols_s[ti, 3 + d:4 + d]
                gc = gc_ref[ti, :]
                sq = sq_s[...]
                for j in range(0, rows, TILE):
                    k, b = k_s[d, j:j + TILE, :], b_s[d, j:j + TILE, :]
                    v_j = vec_ref[d:d + 1, j:j + TILE]
                    teacher = jnp.exp2((dot_nt(q, k) - top_i) * scale) * rinv_i
                    decay = u_i * v_j
                    error = (dot_nt(c, b) * beta) * decay - teacher
                    sq = sq + fold_rows(error * error)
                    held = (error * decay).astype(BF16)
                    gc = gc + dot_nn(held, b)
                    gbt_s[:, j:j + TILE] += dot_nn(ct, held)
                gc_ref[ti, :] = gc
                sq_s[...] = sq

            part = jnp.transpose(gbt_s[...])
            small_ref[d:d + 1, :] = jnp.broadcast_to(
                total_of(part * b_s[d, :, :].astype(F32)) * beta, (1, 128)
            )
            e = exponent_of(part)
            parts[d][0:rows, :] = part * jnp.exp2(14.0 - e)
            parts[d][rows:, :] = jnp.broadcast_to(e, (parts[d].shape[0] - rows, width))

    small_ref[0:1, :] = jnp.broadcast_to(total_of(sq_s[...]), (1, 128))


def own_kernel(
    scale, beta, block_ref, qc_ref, kb_ref, vec_ref, top_ref, rinv_ref, gc_in_ref, small_ref,
    gc_ref, gb_ref, out_ref, q_s, c_s, ct_s, k_s, b_s, gbt_s, cols_s,
):
    block = block_ref[0]
    rows, width = q_s.shape
    n = qc_ref.shape[1] // 2
    q_s[...] = qc_ref[:, 0:n, :].reshape(rows, width)
    c_s[...] = qc_ref[:, n:2 * n, :].reshape(rows, width)
    ct_s[...] = jnp.transpose(c_s[...].astype(F32)).astype(BF16)
    k_s[...] = kb_ref[:, 0:n, :].reshape(rows, width)
    b_s[...] = kb_ref[:, n:2 * n, :].reshape(rows, width)
    cols_s[...] = jnp.transpose(vec_ref[...])
    sq = jnp.zeros((8, 128), F32)
    gbt_s[...] = jnp.zeros(gbt_s.shape, F32)
    for i in range(0, rows, TILE):
        ti = slice(i, i + TILE)
        q, c, ct = q_s[ti, :], c_s[ti, :], ct_s[:, ti]
        top_i = top_ref[ti, 0:1]
        rinv_i = rinv_ref[ti, 0:1]
        sum_i = cols_s[ti, 0:1]
        gc = gc_in_ref[ti, :]
        for j in range(0, i + TILE, TILE):
            k, b = k_s[j:j + TILE, :], b_s[j:j + TILE, :]
            sum_j = vec_ref[0:1, j:j + TILE]
            s = dot_nt(q, k) - top_i
            gap = sum_i - sum_j
            if i == j:
                row = lax.broadcasted_iota(jnp.int32, s.shape, 0)
                col = lax.broadcasted_iota(jnp.int32, s.shape, 1)
                s = jnp.where(col <= row, s, LOWEST)
                gap = jnp.where(col <= row, gap, LOWEST)
            teacher = jnp.exp2(s * scale) * rinv_i
            decay = jnp.exp2(gap * LOG2E)
            error = (dot_nt(c, b) * beta) * decay - teacher
            sq = sq + fold_rows(error * error)
            held = (error * decay).astype(BF16)
            gc = gc + dot_nn(held, b)
            gbt_s[:, j:j + TILE] += dot_nn(ct, held)
        gc_ref[ti, :] = gc
    gb_ref[...] = jnp.transpose(gbt_s[...])
    lane = lax.broadcasted_iota(jnp.int32, (1, 128), 1)
    sums = jnp.where(lane == 3, small_ref[0:1, :] + total_of(sq), 0.0)
    for d in range(1, 4):
        crosses = jnp.logical_and(lane < block, lane >= block - d)
        sums = sums + jnp.where(
            jnp.logical_and(crosses, d <= block), small_ref[d:d + 1, :], 0.0
        )
    out_ref[...] = jnp.broadcast_to(sums, out_ref.shape)


def split_scaled(x, e):
    y = x * jnp.exp2(14.0 - e)
    high = jnp.floor(y * (1.0 / 16.0)) * 16.0
    return high, y - high


def finish_kernel(
    beta, seq_len, block_ref, qc_ref, kb_ref, gc_ref, gb_ref, part1_ref, part2_ref, part3_ref,
    sums_ref, rate_ref, out_ref, gb_s,
):
    block = block_ref[0]
    heads, span, width = qc_ref.shape
    n = span // 2
    rows = heads * n
    gb_s[...] = gb_ref[...]
    for d, part in ((1, part1_ref), (2, part2_ref), (3, part3_ref)):
        @pl.when(block + d <= 3)
        def _(part=part):
            gb_s[...] += part[0:rows, :] * jnp.exp2(part[rows:rows + 1, 0:1] - 14.0)
    gb = gb_s[...]
    gc = gc_ref[...]
    c = qc_ref[:, n:2 * n, :].reshape(rows, width).astype(F32)
    b = kb_ref[:, n:2 * n, :].reshape(rows, width).astype(F32)
    slope = jnp.sum(c * gc - b * gb, axis=1, keepdims=True) * beta
    slope = jnp.broadcast_to(slope, (rows, 128)).reshape(heads, n, 128)
    place = lax.broadcasted_iota(jnp.int32, (heads, n, 128), 1)
    lane3 = lax.broadcasted_iota(jnp.int32, (heads, n, 128), 2)
    slope = jnp.sum(jnp.where(place == lane3, slope, 0.0), axis=1)
    up = lax.broadcasted_iota(jnp.int32, (128, 128), 0)
    across = lax.broadcasted_iota(jnp.int32, (128, 128), 1)
    inside = dot_full(slope, jnp.where(up >= across, 1.0, 0.0).astype(F32))
    down = lax.broadcasted_iota(jnp.int32, (heads, heads), 0)
    right = lax.broadcasted_iota(jnp.int32, (heads, heads), 1)
    whole = jnp.broadcast_to(jnp.sum(slope, axis=1, keepdims=True), (heads, 128))
    behind = dot_full(jnp.where(right > down, 1.0, 0.0).astype(F32), whole)
    lane1 = lax.broadcasted_iota(jnp.int32, (1, 128), 1)
    sums = sums_ref[0:1, :]
    after = jnp.sum(
        jnp.where(jnp.logical_and(lane1 == block, block < 3), sums, 0.0), axis=1, keepdims=True
    )
    error_sq = jnp.sum(jnp.where(lane1 == 3, sums, 0.0), axis=1, keepdims=True)
    norm = jnp.sqrt(error_sq + 1e-06)
    factor = seq_len / norm
    step = (inside + behind + after) * (-(rate_ref[0:1, 0:1] * factor))
    lane = lax.broadcasted_iota(jnp.int32, (heads, 128), 1)
    step = jnp.where(lane < n, step, 0.0)
    gb = gb * (factor * beta)
    gc = gc * (factor * beta)
    eb, ec, es, en = exponent_of(gb), exponent_of(gc), exponent_of(step), exponent_of(norm)
    out_ref[:, 0:n, :] = (gb * jnp.exp2(14.0 - eb)).reshape(heads, n, width)
    out_ref[:, n:2 * n, :] = (gc * jnp.exp2(14.0 - ec)).reshape(heads, n, width)
    high, low = split_scaled(step, es)
    norm_high, norm_low = split_scaled(norm, en)
    extra = jnp.where(lane == 0, eb, 0.0)
    for at, value in ((1, ec), (2, es), (3, norm_high), (4, norm_low), (5, en)):
        extra = jnp.where(lane == at, value, extra)
    out_ref[:, 2 * n:2 * n + 1, :] = high.reshape(heads, 1, 128)
    out_ref[:, 2 * n + 1:2 * n + 2, :] = low.reshape(heads, 1, 128)
    out_ref[:, 2 * n + 2:2 * n + 3, :] = extra.reshape(heads, 1, 128)


def unpack_kernel(x_ref, gb_ref, gc_ref, step_ref, loss_ref):
    heads = x_ref.shape[0]
    n = gb_ref.shape[0]
    extra = x_ref[:, 2 * n + 2:2 * n + 3, :].reshape(heads, 128)
    lane = lax.broadcasted_iota(jnp.int32, (heads, 128), 1)

    def pick(at):
        return jnp.sum(jnp.where(lane == at, extra, 0.0), axis=1, keepdims=True)

    scale_b, scale_c, scale_s = (jnp.exp2(pick(at) - 14.0) for at in range(3))
    norm = (pick(3) + pick(4)) * jnp.exp2(pick(5) - 14.0)
    gb_ref[...] = jnp.swapaxes(x_ref[:, 0:n, :] * scale_b[:, :, None], 0, 1)
    gc_ref[...] = jnp.swapaxes(x_ref[:, n:2 * n, :] * scale_c[:, :, None], 0, 1)
    high = x_ref[:, 2 * n:2 * n + 1, :].reshape(heads, 128)
    low = x_ref[:, 2 * n + 1:2 * n + 2, :].reshape(heads, 128)
    step = jnp.transpose((high + low) * scale_s)
    step_ref[...] = step[0:n, :]
    loss_ref[...] = jnp.broadcast_to(
        jnp.sum(norm, axis=0, keepdims=True) * (1.0 / heads), loss_ref.shape
    )


def call(kernel, out_shape, scratch, count):
    return pl.pallas_call(
        kernel,
        out_shape=out_shape,
        in_specs=[pl.BlockSpec(memory_space=pltpu.SMEM)]
        + [pl.BlockSpec(memory_space=pltpu.VMEM)] * (count - 1),
        out_specs=jax.tree.map(lambda _: pl.BlockSpec(memory_space=pltpu.VMEM), out_shape),
        scratch_shapes=scratch,
        compiler_params=pltpu.CompilerParams(vmem_limit_bytes=VMEM_BYTES),
    )


def shape(*dims, dtype=F32):
    return jax.ShapeDtypeStruct(dims, dtype)


def per_device(queries, keys, b_proj, c_proj, step_size, rate_level):
    n, heads, width = queries.shape
    blocks = lax.axis_size("seq")
    block = lax.axis_index("seq")
    rows = n * heads
    seq_len = rows * blocks
    beta = 2.0 / math.sqrt(width * seq_len)
    scale = LOG2E / math.sqrt(width)

    def to_heads(x):
        return lax.all_to_all(x, "head", split_axis=0, concat_axis=0, tiled=True)

    def flip(x):
        return jnp.swapaxes(x, 0, 1)

    steps = jnp.pad(jnp.transpose(step_size)[:, None, :], ((0, 0), (0, 0), (0, 128 - n % 128 if n % 128 else 0)))
    pad_rows = steps.shape[2] // 128
    steps = steps.reshape(heads, pad_rows, 128)
    kb = to_heads(jnp.concatenate([flip(keys), flip(b_proj), steps], axis=1))
    kb_from = [
        lax.ppermute(kb, "seq", [(i, i + d) for i in range(blocks - d)]) for d in range(1, blocks)
    ]
    qc_mine = jnp.concatenate([flip(queries), flip(c_proj)], axis=1)
    qc_mine, _ = lax.optimization_barrier((qc_mine, kb))
    qc = to_heads(qc_mine)

    rate = jnp.exp2(-0.5 * rate_level.astype(F32))
    dt = jnp.stack([x[:, 2 * n:, :].reshape(heads, -1)[:, :n] for x in [kb] + kb_from])
    local = jnp.cumsum(-rate * dt.reshape(blocks, rows).astype(F32), axis=1)
    total = local[:, -1]
    before = jnp.exp(total[1:, None] - local[1:])
    middle = jnp.stack([jnp.zeros((), F32), total[1], total[1] + total[2]])
    since = jnp.exp(local[0][None] + middle[:, None])
    vec = jnp.concatenate([local[:1], before, since, jnp.zeros((1, rows), F32)], axis=0)

    where = jnp.reshape(block, (1,)).astype(jnp.int32)
    part_rows = rows + 16
    mat = pltpu.VMEM((rows, width), BF16)
    cols = pltpu.VMEM((rows, 8), F32)
    part1, part2, part3, gc, top, rinv, small = call(
        functools.partial(earlier_kernel, scale, beta),
        [shape(part_rows, width)] * 3 + [shape(rows, width)] * 3 + [shape(8, 128)],
        [
            mat, mat, pltpu.VMEM((width, rows), BF16),
            pltpu.VMEM((4, rows, width), BF16), pltpu.VMEM((4, rows, width), BF16),
            pltpu.VMEM((rows, 128), F32), pltpu.VMEM((rows, 128), F32),
            pltpu.VMEM((width, rows), F32), cols, pltpu.VMEM((8, 128), F32),
        ],
        7,
    )(where, qc, kb, *kb_from, vec)
    got = [
        lax.ppermute(part.astype(F16), "seq", [(i, i - d) for i in range(d, blocks)]).astype(F32)
        for d, part in ((1, part1), (2, part2), (3, part3))
    ]
    gc, gb, small = call(
        functools.partial(own_kernel, scale, beta),
        [shape(rows, width), shape(rows, width), shape(8, 128)],
        [
            mat, mat, pltpu.VMEM((width, rows), BF16), mat, mat,
            pltpu.VMEM((width, rows), F32), cols,
        ],
        8,
    )(where, qc, kb, vec, top, rinv, gc, small)
    sums = lax.psum(small, "seq")
    rates = jnp.broadcast_to(rate[None, :], (8, 128))
    packed = call(
        functools.partial(finish_kernel, beta, float(seq_len)),
        shape(heads, 2 * n + 3, width),
        [pltpu.VMEM((rows, width), F32)],
        10,
    )(where, qc, kb, gc, gb, *got, sums, rates)
    back = to_heads(packed.astype(F16)).astype(F32)
    grad_b, grad_c, grad_step, loss = pl.pallas_call(
        unpack_kernel,
        out_shape=[
            shape(n, heads, width), shape(n, heads, width), shape(n, heads), shape(8, 128),
        ],
        compiler_params=pltpu.CompilerParams(vmem_limit_bytes=VMEM_BYTES),
    )(back)
    return grad_b, grad_c, grad_step, loss[0, 0]


def solution(mesh):
    tokens = P(("seq", "head"), None, None)
    return jax.shard_map(
        per_device,
        mesh=mesh,
        in_specs=(tokens, tokens, tokens, tokens, P(("seq", "head"), None), P("head")),
        out_specs=(tokens, tokens, P(("seq", "head"), None), P()),
        check_vma=False,
    )
```

```python
import functools
import math

import jax
import jax.numpy as jnp
from jax import lax
from jax.experimental import pallas as pl
from jax.experimental.pallas import tpu as pltpu
from jax.sharding import PartitionSpec as P

F32 = jnp.float32
BF16 = jnp.bfloat16
F16 = jnp.float16
LOG2E = math.log2(math.e)
TILE = 256
WIDE = 512
OWN = 512
LOWEST = -1e30
VMEM_BYTES = 32 * 1024 * 1024


def dot_nt(a, b):
    return lax.dot_general(a, b, (((1,), (1,)), ((), ())), preferred_element_type=F32)


def dot_nn(a, b):
    return lax.dot_general(a, b, (((1,), (0,)), ((), ())), preferred_element_type=F32)


def dot_full(a, b):
    return lax.dot_general(
        a, b, (((1,), (0,)), ((), ())),
        precision=lax.Precision.HIGHEST, preferred_element_type=F32,
    )


def fold_rows(x):
    rows, cols = x.shape
    x = jnp.sum(x.reshape(rows // 8, 8, cols), axis=0)
    out = x[:, :128]
    for at in range(128, cols, 128):
        out = out + x[:, at:at + 128]
    return out


def total_of(x):
    return jnp.sum(jnp.sum(x, axis=0, keepdims=True), axis=1, keepdims=True)


def exponent_of(x):
    top = jnp.max(jnp.max(jnp.abs(x), axis=0, keepdims=True), axis=1, keepdims=True)
    return jnp.floor(jnp.log2(jnp.maximum(top, 1e-30)))


def sums_rows(log_decay, rows, n):
    heads, lanes = log_decay.shape
    up = lax.broadcasted_iota(jnp.int32, (lanes, lanes), 0)
    across = lax.broadcasted_iota(jnp.int32, (lanes, lanes), 1)
    same = up // n == across // n
    inside = dot_full(log_decay, jnp.where(same & (up <= across), 1.0, 0.0).astype(F32))
    whole = dot_full(log_decay, jnp.where(same, 1.0, 0.0).astype(F32))
    down = lax.broadcasted_iota(jnp.int32, (heads, heads), 0)
    right = lax.broadcasted_iota(jnp.int32, (heads, heads), 1)
    sums = inside + dot_full(jnp.where(right < down, 1.0, 0.0).astype(F32), whole)
    lane = lax.broadcasted_iota(jnp.int32, (lanes, rows), 0)
    place = lax.broadcasted_iota(jnp.int32, (lanes, rows), 1)
    owner = lax.broadcasted_iota(jnp.int32, (heads, rows), 0)
    token = lax.broadcasted_iota(jnp.int32, (heads, rows), 1)
    high = sums.astype(BF16)
    rest = sums - high.astype(F32)
    mid = rest.astype(BF16)
    low = (rest - mid.astype(F32)).astype(BF16)
    terms = jnp.concatenate([high, mid, low], axis=0)
    pick = jnp.where(lane == place % n, 1.0, 0.0).astype(BF16)
    spread = dot_nn(terms, pick)
    spread = spread[0:heads] + spread[heads:2 * heads] + spread[2 * heads:]
    return jnp.sum(jnp.where(token // n == owner, spread, 0.0), axis=0, keepdims=True)


def split_scaled(x, e):
    y = x * jnp.exp2(14.0 - e)
    high = jnp.floor(y * (1.0 / 16.0)) * 16.0
    return high, y - high


def add_stats(s, scale, max_ref, sum_ref, ti, first):
    new = LOWEST if first else max_ref[ti, :]
    size = s.shape[1]
    for g in range(0, size, 128):
        new = jnp.maximum(new, s[:, g:g + 128])
    acc = 0.0 if first else sum_ref[ti, :] * jnp.exp2((max_ref[ti, :] - new) * scale)
    for g in range(0, size, 128):
        acc = acc + jnp.exp2((s[:, g:g + 128] - new) * scale)
    max_ref[ti, :] = new
    sum_ref[ti, :] = acc


def take(ref, at, n):
    heads, _, width = ref.shape
    return ref[:, at * n:(at + 1) * n, :].reshape(heads * n, width)


def pack_kernel(*refs):
    x_ref, y_ref, out_ref = refs[0], refs[1], refs[-1]
    n, heads, _ = x_ref.shape
    out_ref[:, 0:n, :] = jnp.swapaxes(x_ref[...], 0, 1)
    out_ref[:, n:2 * n, :] = jnp.swapaxes(y_ref[...], 0, 1)
    if len(refs) == 4:
        steps = refs[2][...].astype(F32)
        steps = jnp.concatenate([steps, jnp.zeros((128 - n, heads), F32)], axis=0)
        out_ref[:, 2 * n:2 * n + 1, :] = jnp.transpose(steps).reshape(heads, 1, 128).astype(BF16)


def own_stats_kernel(n, scale, level_ref, kq_ref, local_ref, max_ref, sum_ref):
    rows = max_ref.shape[0]
    heads = kq_ref.shape[0]
    k, q = take(kq_ref, 0, n), take(kq_ref, 1, n)
    for at in range(0, rows, TILE):
        ti = slice(at, at + TILE)
        s = dot_nt(q[ti, :], k[0:at + TILE, :])
        row = lax.broadcasted_iota(jnp.int32, s.shape, 0) + at
        col = lax.broadcasted_iota(jnp.int32, s.shape, 1)
        add_stats(jnp.where(col <= row, s, LOWEST), scale, max_ref, sum_ref, ti, True)

    level = jnp.full((1, 1), level_ref[0], jnp.int32).astype(F32)
    steps = kq_ref[:, 2 * n:2 * n + 1, :].astype(F32).reshape(heads, 128)
    local = sums_rows(-jnp.exp2(-0.5 * level) * steps, rows, n)
    local_ref[...] = jnp.broadcast_to(local, local_ref.shape)


def stats_kernel(
    n, scale, block_ref, kq_ref, in1_ref, in2_ref, in3_ref, max_ref, sum_ref,
    local0_ref, local1_ref, local2_ref, local3_ref, out_ref, vec_ref, q_s, k_s, max_s, sum_s,
):
    block = block_ref[0]
    q_s[...] = take(kq_ref, 1, n)
    max_s[...] = max_ref[...]
    sum_s[...] = sum_ref[...]
    for d, in_ref in enumerate((in1_ref, in2_ref, in3_ref)):
        k_s[d + 1, :, :] = take(in_ref, 0, n)

    rows = q_s.shape[0]
    local = [x[0:1, :] for x in (local0_ref, local1_ref, local2_ref, local3_ref)]
    ends = [x[:, rows - 1:rows] for x in local]
    vec_ref[0:1, :] = local[0]
    vec_ref[7:8, :] = jnp.zeros((1, rows), F32)
    for d in range(1, 4):
        nearer, farther = jnp.zeros((1, 1), F32), jnp.zeros((1, 1), F32)
        for g in range(1, d):
            nearer = nearer + ends[g]
        for g in range(d + 1, 4):
            farther = farther + ends[g]
        row_side = block >= d
        v = jnp.where(row_side, ends[d] - local[d], ends[0] - local[0])
        u = jnp.where(row_side, local[0] + nearer, local[d] + farther)
        vec_ref[d:d + 1, :] = jnp.exp2(v * LOG2E)
        vec_ref[3 + d:4 + d, :] = jnp.exp2(u * LOG2E)

    @pl.loop(1, block + 1)
    def _(d):
        add_stats(dot_nt(q_s[...], k_s[d]), scale, max_s, sum_s, slice(None), False)

    top = jnp.max(max_s[...], axis=1, keepdims=True)
    total = jnp.sum(sum_s[...] * jnp.exp2((max_s[...] - top) * scale), axis=1, keepdims=True)
    lane = lax.broadcasted_iota(jnp.int32, (rows, 8), 1)
    out_ref[...] = jnp.transpose(jnp.where(lane == 0, top, 1.0 / total))


def rows_kernel(
    n, scale, beta, block_ref, kq_ref, bc_ref, k1_ref, k2_ref, k3_ref, b1_ref, b2_ref, b3_ref,
    vec_ref, stats_ref, gc_ref, gb_ref, out_ref, q_s, c_s, k_s, b_s, gbt_s, cols_s, u_s, sq_s, cross_s,
):
    block = block_ref[0]
    rows, width = q_s.shape
    k_s[0, :, :] = take(kq_ref, 0, n)
    b_s[0, :, :] = take(bc_ref, 0, n)
    q_s[...] = take(kq_ref, 1, n)
    c_s[...] = take(bc_ref, 1, n)
    ct = jnp.transpose(c_s[...].astype(F32)).astype(BF16)
    for d, (k_ref, b_ref) in enumerate(((k1_ref, b1_ref), (k2_ref, b2_ref), (k3_ref, b3_ref))):
        k_s[d + 1, :, :] = take(k_ref, 0, n)
        b_s[d + 1, :, :] = take(b_ref, 0, n)
    place = lax.broadcasted_iota(jnp.int32, (8, rows), 0)
    vec = vec_ref[...]
    cols_s[...] = jnp.transpose(
        jnp.where(place == 1, stats_ref[0:1, :], jnp.where(place == 2, stats_ref[1:2, :], vec))
    )
    spread = jnp.transpose(vec)
    for d in range(1, 4):
        u_s[d, :, :] = spread[:, 3 + d:4 + d]

    sq = jnp.zeros((8, 128), F32)
    gbt_s[...] = jnp.zeros(gbt_s.shape, F32)
    for i in range(0, rows, OWN):
        ti = slice(i, i + OWN)
        q, c = q_s[ti, :], c_s[ti, :]
        top_i, rinv_i, sum_i = cols_s[ti, 1:2], cols_s[ti, 2:3], cols_s[ti, 0:1]
        gc = 0.0
        for j in range(0, i + OWN, OWN):
            tj = slice(j, j + OWN)
            k, b = k_s[0, tj, :], b_s[0, tj, :]
            s = dot_nt(q, k) - top_i
            gap = sum_i - vec_ref[0:1, tj]
            if i == j:
                row = lax.broadcasted_iota(jnp.int32, s.shape, 0)
                col = lax.broadcasted_iota(jnp.int32, s.shape, 1)
                s = jnp.where(col <= row, s, LOWEST)
                gap = jnp.where(col <= row, gap, LOWEST)
            teacher = jnp.exp2(s * scale) * rinv_i
            decay = jnp.exp2(gap * LOG2E)
            error = (dot_nt(c, b) * beta) * decay - teacher
            sq = sq + fold_rows(error * error)
            held = (error * decay).astype(BF16)
            gc = gc + dot_nn(held, b)
            gbt_s[:, tj] += dot_nn(ct[:, ti], held)
        gc_ref[ti, :] = gc
    gb_ref[...] = jnp.transpose(gbt_s[...])
    sq_s[...] = sq
    cross_s[...] = jnp.zeros(cross_s.shape, F32)
    lane = lax.broadcasted_iota(jnp.int32, (1, 128), 1)

    @pl.loop(1, block + 1)
    def _(d):
        q, c = q_s[...], c_s[...]
        top_i, rinv_i, u_i = cols_s[:, 1:2], cols_s[:, 2:3], u_s[d]
        gc = 0.0
        sq = sq_s[...]
        for j in range(0, rows, WIDE):
            tj = slice(j, j + WIDE)
            k, b = k_s[d, tj, :], b_s[d, tj, :]
            teacher = jnp.exp2((dot_nt(q, k) - top_i) * scale) * rinv_i
            decay = u_i * vec_ref[pl.ds(d, 1), tj]
            error = (dot_nt(c, b) * beta) * decay - teacher
            sq = sq + fold_rows(error * error)
            gc = gc + dot_nn((error * decay).astype(BF16), b)
        cross = total_of(gc * c.astype(F32)) * beta
        cross_s[...] += jnp.where((lane < block) & (lane >= block - d), cross, 0.0)
        gc_ref[...] += gc
        sq_s[...] = sq

    sums = jnp.where(lane == 3, total_of(sq_s[...]), cross_s[...])
    out_ref[...] = jnp.broadcast_to(sums, out_ref.shape)


def cols_kernel(
    n, scale, beta, block_ref, kq_ref, bc_ref, q1_ref, q2_ref, q3_ref, c1_ref, c2_ref, c3_ref,
    vec_ref, st1_ref, st2_ref, st3_ref, gb_in_ref, sums_in_ref, gb_ref, sums_ref,
    k_s, b_s, q_s, c_s, cols_s, gbt_s,
):
    block = block_ref[0]
    rows, width = k_s.shape
    sums_ref[...] = sums_in_ref[...]
    k_s[...] = take(kq_ref, 0, n)
    b_s[...] = take(bc_ref, 0, n)
    place = lax.broadcasted_iota(jnp.int32, (8, rows), 0)
    incoming = ((q1_ref, c1_ref, st1_ref), (q2_ref, c2_ref, st2_ref), (q3_ref, c3_ref, st3_ref))
    for d, (q_ref, c_ref, st_ref) in enumerate(incoming):
        q_s[d + 1, :, :] = take(q_ref, 0, n)
        c_s[d + 1, :, :] = take(c_ref, 0, n)
        cols_s[d + 1, :, :] = jnp.transpose(
            jnp.where(place == 0, st_ref[0:1, :],
                      jnp.where(place == 1, st_ref[1:2, :], vec_ref[4 + d:5 + d, :]))
        )
    gbt_s[...] = jnp.zeros(gbt_s.shape, F32)

    @pl.loop(block + 1, 4)
    def _(d):
        q, c = q_s[d], c_s[d]
        ct = jnp.transpose(c.astype(F32)).astype(BF16)
        top_i, rinv_i, u_i = cols_s[d, :, 0:1], cols_s[d, :, 1:2], cols_s[d, :, 2:3]
        for j in range(0, rows, WIDE):
            tj = slice(j, j + WIDE)
            k, b = k_s[tj, :], b_s[tj, :]
            teacher = jnp.exp2((dot_nt(q, k) - top_i) * scale) * rinv_i
            decay = u_i * vec_ref[pl.ds(d, 1), tj]
            error = (dot_nt(c, b) * beta) * decay - teacher
            gbt_s[:, tj] += dot_nn(ct, (error * decay).astype(BF16))

    gb_ref[...] = gb_in_ref[...] + jnp.transpose(gbt_s[...])


def finish_kernel(
    n, beta, seq_len, block_ref, level_ref, bc_ref, gc_ref, gb_ref,
    sums0_ref, sums1_ref, sums2_ref, sums3_ref, out_ref,
):
    block = block_ref[0]
    heads, _, width = bc_ref.shape
    rows = heads * n
    gb = gb_ref[...]
    gc = gc_ref[...]
    c = take(bc_ref, 1, n).astype(F32)
    b = take(bc_ref, 0, n).astype(F32)
    slope = jnp.sum(c * gc - b * gb, axis=1, keepdims=True) * beta
    slope = jnp.broadcast_to(slope, (rows, 128)).reshape(heads, n, 128)
    place = lax.broadcasted_iota(jnp.int32, (heads, n, 128), 1)
    lane3 = lax.broadcasted_iota(jnp.int32, (heads, n, 128), 2)
    slope = jnp.sum(jnp.where(place == lane3 % n, slope, 0.0), axis=1)
    up = lax.broadcasted_iota(jnp.int32, (128, 128), 0)
    across = lax.broadcasted_iota(jnp.int32, (128, 128), 1)
    same = up // n == across // n
    inside = dot_full(slope, jnp.where(same & (up >= across), 1.0, 0.0).astype(F32))
    whole = dot_full(slope, jnp.where(same, 1.0, 0.0).astype(F32))
    down = lax.broadcasted_iota(jnp.int32, (heads, heads), 0)
    right = lax.broadcasted_iota(jnp.int32, (heads, heads), 1)
    behind = dot_full(jnp.where(right > down, 1.0, 0.0).astype(F32), whole)
    lane1 = lax.broadcasted_iota(jnp.int32, (1, 128), 1)
    sums = (sums0_ref[0:1, :] + sums1_ref[0:1, :]) + (sums2_ref[0:1, :] + sums3_ref[0:1, :])
    after = jnp.sum(
        jnp.where(jnp.logical_and(lane1 == block, block < 3), sums, 0.0), axis=1, keepdims=True
    )
    error_sq = jnp.sum(jnp.where(lane1 == 3, sums, 0.0), axis=1, keepdims=True)
    norm = jnp.sqrt(error_sq + 1e-06)
    factor = seq_len / norm
    rate = jnp.exp2(-0.5 * jnp.full((1, 1), level_ref[0], jnp.int32).astype(F32))
    step = (inside + behind + after) * (-(rate * factor))
    lane = lax.broadcasted_iota(jnp.int32, (heads, 128), 1)
    gb = gb * (factor * beta)
    gc = gc * (factor * beta)
    eb, ec, es, en = exponent_of(gb), exponent_of(gc), exponent_of(step), exponent_of(norm)
    out_ref[:, 0:n, :] = (gb * jnp.exp2(14.0 - eb)).reshape(heads, n, width)
    out_ref[:, n:2 * n, :] = (gc * jnp.exp2(14.0 - ec)).reshape(heads, n, width)
    high, low = split_scaled(step, es)
    norm_high, norm_low = split_scaled(norm, en)
    last = jnp.where(lane < n, high, low)
    for at, value in enumerate((eb, ec, es, norm_high, norm_low, en)):
        last = jnp.where(lane == 2 * n + at, value, last)
    out_ref[:, 2 * n:2 * n + 1, :] = last.reshape(heads, 1, 128)


def unpack_kernel(x_ref, gb_ref, gc_ref, step_ref, loss_ref):
    heads = x_ref.shape[0]
    n = gb_ref.shape[0]
    last = x_ref[:, 2 * n:2 * n + 1, :].reshape(heads, 128)
    lane = lax.broadcasted_iota(jnp.int32, (heads, 128), 1)

    def pick(at):
        return jnp.sum(jnp.where(lane == 2 * n + at, last, 0.0), axis=1, keepdims=True)

    scale_b, scale_c, scale_s = (jnp.exp2(pick(at) - 14.0) for at in range(3))
    norm = (pick(3) + pick(4)) * jnp.exp2(pick(5) - 14.0)
    gb_ref[...] = jnp.swapaxes(x_ref[:, 0:n, :] * scale_b[:, :, None], 0, 1)
    gc_ref[...] = jnp.swapaxes(x_ref[:, n:2 * n, :] * scale_c[:, :, None], 0, 1)
    step = jnp.transpose(last * scale_s)
    step_ref[...] = step[0:n, :] + step[n:2 * n, :]
    loss_ref[...] = jnp.sum(norm, axis=0, keepdims=True) * (1.0 / heads)


def call(kernel, out_shape, scratch, scalars, count):
    return pl.pallas_call(
        kernel,
        out_shape=out_shape,
        in_specs=[pl.BlockSpec(memory_space=pltpu.SMEM)] * scalars
        + [pl.BlockSpec(memory_space=pltpu.VMEM)] * (count - scalars),
        out_specs=jax.tree.map(lambda _: pl.BlockSpec(memory_space=pltpu.VMEM), out_shape),
        scratch_shapes=scratch,
        compiler_params=pltpu.CompilerParams(vmem_limit_bytes=VMEM_BYTES),
    )


def shape(*dims, dtype=F32):
    return jax.ShapeDtypeStruct(dims, dtype)


def near(*dims, dtype=F32):
    return pltpu.VMEM(dims, dtype)


def held_near(x):
    return pltpu.with_memory_space_constraint(x, pltpu.VMEM)


def per_device(queries, keys, b_proj, c_proj, step_size, rate_level):
    n, heads, width = queries.shape
    blocks = lax.axis_size("seq")
    block = lax.axis_index("seq")
    rows = n * heads
    seq_len = rows * blocks
    beta = 2.0 / math.sqrt(width * seq_len)
    scale = LOG2E / math.sqrt(width)

    def to_heads(x):
        return lax.all_to_all(x, "head", split_axis=0, concat_axis=0, tiled=True)

    def around(x):
        return [
            lax.ppermute(x, "seq", [(i, (i + d) % blocks) for i in range(blocks)])
            for d in range(1, blocks)
        ]

    def exchange(pair):
        mine, after = pair[:, 0:n], pair[:, n:2 * n]
        return [
            held_near(
                lax.ppermute(
                    jnp.where(block + d < blocks, mine, after),
                    "seq", [(i, (i + d) % blocks) for i in range(blocks)],
                )
            )
            for d in range(1, blocks)
        ]

    kq = to_heads(
        call(pack_kernel, near(heads, 2 * n + 1, width, dtype=BF16), [], 0, 3)(
            keys, queries, step_size
        )
    )
    bc = call(pack_kernel, near(heads, 2 * n, width, dtype=BF16), [], 0, 2)(b_proj, c_proj)
    bc, kq = lax.optimization_barrier((bc, kq))
    bc = to_heads(bc)
    kq_from, bc_from = exchange(kq), exchange(bc)
    kq, bc = held_near(kq), held_near(bc)
    where = jnp.reshape(block, (1,)).astype(jnp.int32)
    mat = pltpu.VMEM((rows, width), BF16)
    mats = pltpu.VMEM((blocks, rows, width), BF16)
    flat = pltpu.VMEM((width, rows), F32)
    state = pltpu.VMEM((rows, 128), F32)
    local, top, total = call(
        functools.partial(own_stats_kernel, n, scale),
        [near(8, rows), near(rows, 128), near(rows, 128)], [], 1, 2,
    )(rate_level, kq)
    local_from = [held_near(x) for x in around(local)]
    stats, vec = call(
        functools.partial(stats_kernel, n, scale), [near(8, rows), near(8, rows)],
        [mat, mats, state, state], 1, 11,
    )(where, kq, *kq_from, top, total, local, *local_from)
    stats_from = [held_near(x) for x in around(stats)]
    gc, gb, sums = call(
        functools.partial(rows_kernel, n, scale, beta),
        [near(rows, width), near(rows, width), near(8, 128)],
        [
            mat, mat, mats, mats, flat, pltpu.VMEM((rows, 8), F32),
            pltpu.VMEM((4, rows, 1), F32), pltpu.VMEM((8, 128), F32), pltpu.VMEM((1, 128), F32),
        ],
        1, 11,
    )(where, kq, bc, *kq_from, *bc_from, vec, stats)
    gb, sums = call(
        functools.partial(cols_kernel, n, scale, beta),
        [near(rows, width), near(8, 128)],
        [mat, mat, mats, mats, pltpu.VMEM((4, rows, 8), F32), flat],
        1, 15,
    )(where, kq, bc, *kq_from, *bc_from, vec, *stats_from, gb, sums)
    sums_from = [held_near(x) for x in around(sums)]
    packed = call(
        functools.partial(finish_kernel, n, beta, float(seq_len)),
        near(heads, 2 * n + 1, width), [], 2, 9,
    )(where, rate_level, bc, gc, gb, sums, *sums_from)
    back = to_heads(packed.astype(F16)).astype(F32)
    grad_b, grad_c, grad_step, loss = pl.pallas_call(
        unpack_kernel,
        out_shape=[
            shape(n, heads, width), shape(n, heads, width), shape(n, heads), shape(1, 1),
        ],
        compiler_params=pltpu.CompilerParams(vmem_limit_bytes=VMEM_BYTES),
    )(held_near(back))
    return grad_b, grad_c, grad_step, jnp.reshape(loss, ())


def solution(mesh):
    tokens = P(("seq", "head"), None, None)
    return jax.shard_map(
        per_device,
        mesh=mesh,
        in_specs=(tokens, tokens, tokens, tokens, P(("seq", "head"), None), P("head")),
        out_specs=(tokens, tokens, P(("seq", "head"), None), P()),
        check_vma=False,
    )
```

```python
import functools
import math

import jax
import jax.numpy as jnp
from jax import lax
from jax.experimental import pallas as pl
from jax.experimental.pallas import tpu as pltpu
from jax.sharding import PartitionSpec as P

F32 = jnp.float32
BF16 = jnp.bfloat16
F16 = jnp.float16
LOG2E = math.log2(math.e)
TILE = 256
WIDE = 512
OWN = 512
LOWEST = -1e30
VMEM_BYTES = 32 * 1024 * 1024


def dot_nt(a, b):
    return lax.dot_general(a, b, (((1,), (1,)), ((), ())), preferred_element_type=F32)


def dot_nn(a, b):
    return lax.dot_general(a, b, (((1,), (0,)), ((), ())), preferred_element_type=F32)


def dot_full(a, b):
    return lax.dot_general(
        a, b, (((1,), (0,)), ((), ())),
        precision=lax.Precision.HIGHEST, preferred_element_type=F32,
    )


def fold_rows(x):
    rows, cols = x.shape
    x = jnp.sum(x.reshape(rows // 8, 8, cols), axis=0)
    out = x[:, :128]
    for at in range(128, cols, 128):
        out = out + x[:, at:at + 128]
    return out


def total_of(x):
    return jnp.sum(jnp.sum(x, axis=0, keepdims=True), axis=1, keepdims=True)


def exponent_of(x):
    top = jnp.max(jnp.max(jnp.abs(x), axis=0, keepdims=True), axis=1, keepdims=True)
    return jnp.floor(jnp.log2(jnp.maximum(top, 1e-30)))


def sums_rows(log_decay, rows, n):
    heads, lanes = log_decay.shape
    up = lax.broadcasted_iota(jnp.int32, (lanes, lanes), 0)
    across = lax.broadcasted_iota(jnp.int32, (lanes, lanes), 1)
    same = up // n == across // n
    inside = dot_full(log_decay, jnp.where(same & (up <= across), 1.0, 0.0).astype(F32))
    whole = dot_full(log_decay, jnp.where(same, 1.0, 0.0).astype(F32))
    down = lax.broadcasted_iota(jnp.int32, (heads, heads), 0)
    right = lax.broadcasted_iota(jnp.int32, (heads, heads), 1)
    sums = inside + dot_full(jnp.where(right < down, 1.0, 0.0).astype(F32), whole)
    lane = lax.broadcasted_iota(jnp.int32, (lanes, rows), 0)
    place = lax.broadcasted_iota(jnp.int32, (lanes, rows), 1)
    owner = lax.broadcasted_iota(jnp.int32, (heads, rows), 0)
    token = lax.broadcasted_iota(jnp.int32, (heads, rows), 1)
    high = sums.astype(BF16)
    rest = sums - high.astype(F32)
    mid = rest.astype(BF16)
    low = (rest - mid.astype(F32)).astype(BF16)
    terms = jnp.concatenate([high, mid, low], axis=0)
    pick = jnp.where(lane == place % n, 1.0, 0.0).astype(BF16)
    spread = dot_nn(terms, pick)
    spread = spread[0:heads] + spread[heads:2 * heads] + spread[2 * heads:]
    return jnp.sum(jnp.where(token // n == owner, spread, 0.0), axis=0, keepdims=True)


def split_scaled(x, e):
    y = x * jnp.exp2(14.0 - e)
    high = jnp.floor(y * (1.0 / 16.0)) * 16.0
    return high, y - high


def add_stats(s, scale, max_ref, sum_ref, ti, first):
    new = LOWEST if first else max_ref[ti, :]
    size = s.shape[1]
    for g in range(0, size, 128):
        new = jnp.maximum(new, s[:, g:g + 128])
    acc = 0.0 if first else sum_ref[ti, :] * jnp.exp2((max_ref[ti, :] - new) * scale)
    for g in range(0, size, 128):
        acc = acc + jnp.exp2((s[:, g:g + 128] - new) * scale)
    max_ref[ti, :] = new
    sum_ref[ti, :] = acc


def take(ref, at, n):
    heads, _, width = ref.shape
    return ref[:, at * n:(at + 1) * n, :].reshape(heads * n, width)


def pack_kernel(*refs):
    parts, steps_ref, out_ref = refs[:-2], refs[-2], refs[-1]
    n, heads, _ = parts[0].shape
    for at, ref in enumerate(parts):
        out_ref[:, at * n:(at + 1) * n, :] = jnp.swapaxes(ref[...], 0, 1)
    steps = jnp.concatenate([steps_ref[...].astype(F32), jnp.zeros((128 - n, heads), F32)], axis=0)
    last = len(parts) * n
    out_ref[:, last:last + 1, :] = jnp.transpose(steps).reshape(heads, 1, 128).astype(BF16)


def own_stats_kernel(n, scale, level_ref, own_ref, local_ref, max_ref, sum_ref):
    rows = max_ref.shape[0]
    heads = own_ref.shape[0]
    k, q = take(own_ref, 0, n), take(own_ref, 1, n)
    for at in range(0, rows, TILE):
        ti = slice(at, at + TILE)
        s = dot_nt(q[ti, :], k[0:at + TILE, :])
        row = lax.broadcasted_iota(jnp.int32, s.shape, 0) + at
        col = lax.broadcasted_iota(jnp.int32, s.shape, 1)
        add_stats(jnp.where(col <= row, s, LOWEST), scale, max_ref, sum_ref, ti, True)

    level = jnp.full((1, 1), level_ref[0], jnp.int32).astype(F32)
    steps = own_ref[:, 4 * n:4 * n + 1, :].astype(F32).reshape(heads, 128)
    local = sums_rows(-jnp.exp2(-0.5 * level) * steps, rows, n)
    local_ref[...] = jnp.broadcast_to(local, local_ref.shape)


def stats_kernel(
    n, scale, block_ref, own_ref, in1_ref, in2_ref, in3_ref, local_ref, max_ref, sum_ref,
    out_ref, q_s, k_s, max_s, sum_s,
):
    block = block_ref[0]
    rows = q_s.shape[0]
    q_s[...] = take(own_ref, 1, n)
    max_s[...] = max_ref[...]
    sum_s[...] = sum_ref[...]
    for d, in_ref in enumerate((in1_ref, in2_ref, in3_ref)):
        k_s[d + 1, :, :] = take(in_ref, 0, n)

    @pl.loop(1, block + 1)
    def _(d):
        add_stats(dot_nt(q_s[...], k_s[d]), scale, max_s, sum_s, slice(None), False)

    top = jnp.max(max_s[...], axis=1, keepdims=True)
    total = jnp.sum(sum_s[...] * jnp.exp2((max_s[...] - top) * scale), axis=1, keepdims=True)
    lane = lax.broadcasted_iota(jnp.int32, (rows, 8), 1)
    out_ref[...] = jnp.transpose(jnp.where(lane == 0, top, 1.0 / total))
    out_ref[2:3, :] = local_ref[0:1, :]


def fill_vec(block, stats_refs, vec_ref):
    local = [x[2:3, :] for x in stats_refs]
    rows = vec_ref.shape[1]
    ends = [x[:, rows - 1:rows] for x in local]
    vec_ref[0:1, :] = local[0]
    vec_ref[7:8, :] = jnp.zeros((1, rows), F32)
    for d in range(1, 4):
        nearer, farther = jnp.zeros((1, 1), F32), jnp.zeros((1, 1), F32)
        for g in range(1, d):
            nearer = nearer + ends[g]
        for g in range(d + 1, 4):
            farther = farther + ends[g]
        row_side = block >= d
        v = jnp.where(row_side, ends[d] - local[d], ends[0] - local[0])
        u = jnp.where(row_side, local[0] + nearer, local[d] + farther)
        vec_ref[d:d + 1, :] = jnp.exp2(v * LOG2E)
        vec_ref[3 + d:4 + d, :] = jnp.exp2(u * LOG2E)


def own_kernel(
    n, scale, beta, own_ref, stats_ref, gc_ref, gb_ref, sq_ref, gbt_s, cols_s,
):
    rows = gc_ref.shape[0]
    k_all, q_all, b_all, c_all = (take(own_ref, at, n) for at in range(4))
    ct = jnp.transpose(c_all.astype(F32)).astype(BF16)
    cols_s[...] = jnp.transpose(stats_ref[...])
    sq = jnp.zeros((8, 128), F32)
    gbt_s[...] = jnp.zeros(gbt_s.shape, F32)
    for i in range(0, rows, OWN):
        ti = slice(i, i + OWN)
        q, c = q_all[ti, :], c_all[ti, :]
        top_i, rinv_i, sum_i = cols_s[ti, 0:1], cols_s[ti, 1:2], cols_s[ti, 2:3]
        gc = 0.0
        for j in range(0, i + OWN, OWN):
            tj = slice(j, j + OWN)
            k, b = k_all[tj, :], b_all[tj, :]
            s = dot_nt(q, k) - top_i
            gap = sum_i - stats_ref[2:3, tj]
            if i == j:
                row = lax.broadcasted_iota(jnp.int32, s.shape, 0)
                col = lax.broadcasted_iota(jnp.int32, s.shape, 1)
                s = jnp.where(col <= row, s, LOWEST)
                gap = jnp.where(col <= row, gap, LOWEST)
            teacher = jnp.exp2(s * scale) * rinv_i
            decay = jnp.exp2(gap * LOG2E)
            error = (dot_nt(c, b) * beta) * decay - teacher
            sq = sq + fold_rows(error * error)
            held = (error * decay).astype(BF16)
            gc = gc + dot_nn(held, b)
            gbt_s[:, tj] += dot_nn(ct[:, ti], held)
        gc_ref[ti, :] = gc
    gb_ref[...] = jnp.transpose(gbt_s[...])
    sq_ref[...] = sq


def rows_kernel(
    n, scale, beta, block_ref, own_ref, k1_ref, k2_ref, k3_ref, b1_ref, b2_ref, b3_ref,
    stats_ref, st1_ref, st2_ref, st3_ref, gc_in_ref, sq_in_ref, gc_ref, out_ref, vec_ref,
    q_s, c_s, k_s, b_s, cols_s, u_s, sq_s, cross_s,
):
    block = block_ref[0]
    rows, width = q_s.shape
    fill_vec(block, (stats_ref, st1_ref, st2_ref, st3_ref), vec_ref)
    q_s[...] = take(own_ref, 1, n)
    c_s[...] = take(own_ref, 3, n)
    for d, (k_ref, b_ref) in enumerate(((k1_ref, b1_ref), (k2_ref, b2_ref), (k3_ref, b3_ref))):
        k_s[d + 1, :, :] = take(k_ref, 0, n)
        b_s[d + 1, :, :] = take(b_ref, 0, n)
    cols_s[...] = jnp.transpose(stats_ref[...])
    spread = jnp.transpose(vec_ref[...])
    for d in range(1, 4):
        u_s[d, :, :] = spread[:, 3 + d:4 + d]
    gc_ref[...] = gc_in_ref[...]
    sq_s[...] = sq_in_ref[...]
    cross_s[...] = jnp.zeros(cross_s.shape, F32)
    lane = lax.broadcasted_iota(jnp.int32, (1, 128), 1)

    @pl.loop(1, block + 1)
    def _(d):
        q, c = q_s[...], c_s[...]
        top_i, rinv_i, u_i = cols_s[:, 0:1], cols_s[:, 1:2], u_s[d]
        gc = 0.0
        sq = sq_s[...]
        for j in range(0, rows, WIDE):
            tj = slice(j, j + WIDE)
            k, b = k_s[d, tj, :], b_s[d, tj, :]
            teacher = jnp.exp2((dot_nt(q, k) - top_i) * scale) * rinv_i
            decay = u_i * vec_ref[pl.ds(d, 1), tj]
            error = (dot_nt(c, b) * beta) * decay - teacher
            sq = sq + fold_rows(error * error)
            gc = gc + dot_nn((error * decay).astype(BF16), b)
        cross = total_of(gc * c.astype(F32)) * beta
        cross_s[...] += jnp.where((lane < block) & (lane >= block - d), cross, 0.0)
        gc_ref[...] += gc
        sq_s[...] = sq

    sums = jnp.where(lane == 3, total_of(sq_s[...]), cross_s[...])
    out_ref[...] = jnp.broadcast_to(sums, out_ref.shape)


def cols_kernel(
    n, scale, beta, block_ref, own_ref, q1_ref, q2_ref, q3_ref, c1_ref, c2_ref, c3_ref,
    vec_ref, st1_ref, st2_ref, st3_ref, gb_in_ref, sums_in_ref, gb_ref, sums_ref,
    k_s, b_s, q_s, c_s, cols_s, gbt_s,
):
    block = block_ref[0]
    rows, width = k_s.shape
    sums_ref[...] = sums_in_ref[...]
    k_s[...] = take(own_ref, 0, n)
    b_s[...] = take(own_ref, 2, n)
    place = lax.broadcasted_iota(jnp.int32, (8, rows), 0)
    incoming = ((q1_ref, c1_ref, st1_ref), (q2_ref, c2_ref, st2_ref), (q3_ref, c3_ref, st3_ref))
    for d, (q_ref, c_ref, st_ref) in enumerate(incoming):
        q_s[d + 1, :, :] = take(q_ref, 0, n)
        c_s[d + 1, :, :] = take(c_ref, 0, n)
        cols_s[d + 1, :, :] = jnp.transpose(
            jnp.where(place == 0, st_ref[0:1, :],
                      jnp.where(place == 1, st_ref[1:2, :], vec_ref[4 + d:5 + d, :]))
        )
    gbt_s[...] = jnp.zeros(gbt_s.shape, F32)

    @pl.loop(block + 1, 4)
    def _(d):
        q, c = q_s[d], c_s[d]
        ct = jnp.transpose(c.astype(F32)).astype(BF16)
        top_i, rinv_i, u_i = cols_s[d, :, 0:1], cols_s[d, :, 1:2], cols_s[d, :, 2:3]
        for j in range(0, rows, WIDE):
            tj = slice(j, j + WIDE)
            k, b = k_s[tj, :], b_s[tj, :]
            teacher = jnp.exp2((dot_nt(q, k) - top_i) * scale) * rinv_i
            decay = u_i * vec_ref[pl.ds(d, 1), tj]
            error = (dot_nt(c, b) * beta) * decay - teacher
            gbt_s[:, tj] += dot_nn(ct, (error * decay).astype(BF16))

    gb_ref[...] = gb_in_ref[...] + jnp.transpose(gbt_s[...])


def finish_kernel(
    n, beta, seq_len, block_ref, level_ref, own_ref, gc_ref, gb_ref,
    sums0_ref, sums1_ref, sums2_ref, sums3_ref, out_ref,
):
    block = block_ref[0]
    heads, _, width = own_ref.shape
    rows = heads * n
    gb = gb_ref[...]
    gc = gc_ref[...]
    c = take(own_ref, 3, n).astype(F32)
    b = take(own_ref, 2, n).astype(F32)
    slope = jnp.sum(c * gc - b * gb, axis=1, keepdims=True) * beta
    slope = jnp.broadcast_to(slope, (rows, 128)).reshape(heads, n, 128)
    place = lax.broadcasted_iota(jnp.int32, (heads, n, 128), 1)
    lane3 = lax.broadcasted_iota(jnp.int32, (heads, n, 128), 2)
    slope = jnp.sum(jnp.where(place == lane3 % n, slope, 0.0), axis=1)
    up = lax.broadcasted_iota(jnp.int32, (128, 128), 0)
    across = lax.broadcasted_iota(jnp.int32, (128, 128), 1)
    same = up // n == across // n
    inside = dot_full(slope, jnp.where(same & (up >= across), 1.0, 0.0).astype(F32))
    whole = dot_full(slope, jnp.where(same, 1.0, 0.0).astype(F32))
    down = lax.broadcasted_iota(jnp.int32, (heads, heads), 0)
    right = lax.broadcasted_iota(jnp.int32, (heads, heads), 1)
    behind = dot_full(jnp.where(right > down, 1.0, 0.0).astype(F32), whole)
    lane1 = lax.broadcasted_iota(jnp.int32, (1, 128), 1)
    sums = (sums0_ref[0:1, :] + sums1_ref[0:1, :]) + (sums2_ref[0:1, :] + sums3_ref[0:1, :])
    after = jnp.sum(
        jnp.where(jnp.logical_and(lane1 == block, block < 3), sums, 0.0), axis=1, keepdims=True
    )
    error_sq = jnp.sum(jnp.where(lane1 == 3, sums, 0.0), axis=1, keepdims=True)
    norm = jnp.sqrt(error_sq + 1e-06)
    factor = seq_len / norm
    rate = jnp.exp2(-0.5 * jnp.full((1, 1), level_ref[0], jnp.int32).astype(F32))
    step = (inside + behind + after) * (-(rate * factor))
    lane = lax.broadcasted_iota(jnp.int32, (heads, 128), 1)
    gb = gb * (factor * beta)
    gc = gc * (factor * beta)
    eb, ec, es, en = exponent_of(gb), exponent_of(gc), exponent_of(step), exponent_of(norm)
    out_ref[:, 0:n, :] = (gb * jnp.exp2(14.0 - eb)).reshape(heads, n, width)
    out_ref[:, n:2 * n, :] = (gc * jnp.exp2(14.0 - ec)).reshape(heads, n, width)
    high, low = split_scaled(step, es)
    norm_high, norm_low = split_scaled(norm, en)
    last = jnp.where(lane < n, high, low)
    for at, value in enumerate((eb, ec, es, norm_high, norm_low, en)):
        last = jnp.where(lane == 2 * n + at, value, last)
    out_ref[:, 2 * n:2 * n + 1, :] = last.reshape(heads, 1, 128)


def unpack_kernel(x_ref, gb_ref, gc_ref, step_ref, loss_ref):
    heads = x_ref.shape[0]
    n = gb_ref.shape[0]
    last = x_ref[:, 2 * n:2 * n + 1, :].reshape(heads, 128)
    lane = lax.broadcasted_iota(jnp.int32, (heads, 128), 1)

    def pick(at):
        return jnp.sum(jnp.where(lane == 2 * n + at, last, 0.0), axis=1, keepdims=True)

    scale_b, scale_c, scale_s = (jnp.exp2(pick(at) - 14.0) for at in range(3))
    norm = (pick(3) + pick(4)) * jnp.exp2(pick(5) - 14.0)
    gb_ref[...] = jnp.swapaxes(x_ref[:, 0:n, :] * scale_b[:, :, None], 0, 1)
    gc_ref[...] = jnp.swapaxes(x_ref[:, n:2 * n, :] * scale_c[:, :, None], 0, 1)
    step = jnp.transpose(last * scale_s)
    step_ref[...] = step[0:n, :] + step[n:2 * n, :]
    loss_ref[...] = jnp.sum(norm, axis=0, keepdims=True) * (1.0 / heads)


def call(kernel, out_shape, scratch, scalars, count):
    return pl.pallas_call(
        kernel,
        out_shape=out_shape,
        in_specs=[pl.BlockSpec(memory_space=pltpu.SMEM)] * scalars
        + [pl.BlockSpec(memory_space=pltpu.VMEM)] * (count - scalars),
        out_specs=jax.tree.map(lambda _: pl.BlockSpec(memory_space=pltpu.VMEM), out_shape),
        scratch_shapes=scratch,
        compiler_params=pltpu.CompilerParams(vmem_limit_bytes=VMEM_BYTES),
    )


def shape(*dims, dtype=F32):
    return jax.ShapeDtypeStruct(dims, dtype)


def near(*dims, dtype=F32):
    return pltpu.VMEM(dims, dtype)


def held_near(x):
    return pltpu.with_memory_space_constraint(x, pltpu.VMEM)


def per_device(queries, keys, b_proj, c_proj, step_size, rate_level):
    n, heads, width = queries.shape
    blocks = lax.axis_size("seq")
    block = lax.axis_index("seq")
    rows = n * heads
    seq_len = rows * blocks
    beta = 2.0 / math.sqrt(width * seq_len)
    scale = LOG2E / math.sqrt(width)

    def to_heads(x):
        return lax.all_to_all(x, "head", split_axis=0, concat_axis=0, tiled=True)

    def around(x):
        return [
            lax.ppermute(x, "seq", [(i, (i + d) % blocks) for i in range(blocks)])
            for d in range(1, blocks)
        ]

    def exchange(pair):
        mine, after = pair[:, 0:n], pair[:, n:2 * n]
        return [
            held_near(
                lax.ppermute(
                    jnp.where(block + d < blocks, mine, after),
                    "seq", [(i, (i + d) % blocks) for i in range(blocks)],
                )
            )
            for d in range(1, blocks)
        ]

    inputs = [
        pltpu.with_memory_space_constraint(x, pltpu.HBM)
        for x in (keys, queries, b_proj, c_proj, step_size)
    ]
    arrived = to_heads(
        call(pack_kernel, near(heads, 4 * n + 1, width, dtype=BF16), [], 0, 5)(*inputs)
    )
    kq_from = exchange(arrived[:, 0:2 * n])
    own = held_near(arrived)
    where = jnp.reshape(block, (1,)).astype(jnp.int32)
    mat = pltpu.VMEM((rows, width), BF16)
    mats = pltpu.VMEM((blocks, rows, width), BF16)
    flat = pltpu.VMEM((width, rows), F32)
    state = pltpu.VMEM((rows, 128), F32)
    local, top, total = call(
        functools.partial(own_stats_kernel, n, scale),
        [near(8, rows), near(rows, 128), near(rows, 128)], [], 1, 2,
    )(rate_level, own)
    bc, local = lax.optimization_barrier((arrived[:, 2 * n:4 * n], local))
    bc_from = exchange(bc)
    stats = call(
        functools.partial(stats_kernel, n, scale), near(8, rows), [mat, mats, state, state], 1, 8,
    )(where, own, *kq_from, local, top, total)
    stats_from = [held_near(x) for x in around(stats)]
    gc, gb, sq = call(
        functools.partial(own_kernel, n, scale, beta),
        [near(rows, width), near(rows, width), near(8, 128)],
        [flat, pltpu.VMEM((rows, 8), F32)], 0, 2,
    )(own, stats)
    gc, sums, vec = call(
        functools.partial(rows_kernel, n, scale, beta),
        [near(rows, width), near(8, 128), near(8, rows)],
        [
            mat, mat, mats, mats, pltpu.VMEM((rows, 8), F32),
            pltpu.VMEM((4, rows, 1), F32), pltpu.VMEM((8, 128), F32), pltpu.VMEM((1, 128), F32),
        ],
        1, 14,
    )(where, own, *kq_from, *bc_from, stats, *stats_from, gc, sq)
    gb, sums = call(
        functools.partial(cols_kernel, n, scale, beta),
        [near(rows, width), near(8, 128)],
        [mat, mat, mats, mats, pltpu.VMEM((4, rows, 8), F32), flat],
        1, 14,
    )(where, own, *kq_from, *bc_from, vec, *stats_from, gb, sums)
    sums_from = [held_near(x) for x in around(sums)]
    packed = call(
        functools.partial(finish_kernel, n, beta, float(seq_len)),
        near(heads, 2 * n + 1, width), [], 2, 9,
    )(where, rate_level, own, gc, gb, sums, *sums_from)
    back = to_heads(packed.astype(F16)).astype(F32)
    grad_b, grad_c, grad_step, loss = pl.pallas_call(
        unpack_kernel,
        out_shape=[
            shape(n, heads, width), shape(n, heads, width), shape(n, heads), shape(1, 1),
        ],
        compiler_params=pltpu.CompilerParams(vmem_limit_bytes=VMEM_BYTES),
    )(held_near(back))
    return grad_b, grad_c, grad_step, jnp.reshape(loss, ())


def solution(mesh):
    tokens = P(("seq", "head"), None, None)
    return jax.shard_map(
        per_device,
        mesh=mesh,
        in_specs=(tokens, tokens, tokens, tokens, P(("seq", "head"), None), P("head")),
        out_specs=(tokens, tokens, P(("seq", "head"), None), P()),
        check_vma=False,
    )
```

```python
import functools
import math

import jax
import jax.numpy as jnp
from jax import lax
from jax.experimental import pallas as pl
from jax.experimental.pallas import tpu as pltpu
from jax.sharding import PartitionSpec as P

F32 = jnp.float32
BF16 = jnp.bfloat16
F16 = jnp.float16
LOG2E = math.log2(math.e)
TILE = 256
TALL = 512
WIDE = 512
OWN = 512
LOWEST = -1e30
VMEM_BYTES = 32 * 1024 * 1024


def dot_nt(a, b):
    return lax.dot_general(a, b, (((1,), (1,)), ((), ())), preferred_element_type=F32)


def dot_nn(a, b):
    return lax.dot_general(a, b, (((1,), (0,)), ((), ())), preferred_element_type=F32)


def dot_full(a, b):
    return lax.dot_general(
        a, b, (((1,), (0,)), ((), ())),
        precision=lax.Precision.HIGHEST, preferred_element_type=F32,
    )


def fold_rows(x):
    rows, cols = x.shape
    x = jnp.sum(x.reshape(rows // 8, 8, cols), axis=0)
    out = x[:, :128]
    for at in range(128, cols, 128):
        out = out + x[:, at:at + 128]
    return out


def total_of(x):
    return jnp.sum(jnp.sum(x, axis=0, keepdims=True), axis=1, keepdims=True)


def exponent_of(x):
    top = jnp.max(jnp.max(jnp.abs(x), axis=0, keepdims=True), axis=1, keepdims=True)
    return jnp.floor(jnp.log2(jnp.maximum(top, 1e-30)))


def sums_rows(log_decay, rows, n):
    heads, lanes = log_decay.shape
    up = lax.broadcasted_iota(jnp.int32, (lanes, lanes), 0)
    across = lax.broadcasted_iota(jnp.int32, (lanes, lanes), 1)
    same = up // n == across // n
    inside = dot_full(log_decay, jnp.where(same & (up <= across), 1.0, 0.0).astype(F32))
    whole = dot_full(log_decay, jnp.where(same, 1.0, 0.0).astype(F32))
    down = lax.broadcasted_iota(jnp.int32, (heads, heads), 0)
    right = lax.broadcasted_iota(jnp.int32, (heads, heads), 1)
    sums = inside + dot_full(jnp.where(right < down, 1.0, 0.0).astype(F32), whole)
    lane = lax.broadcasted_iota(jnp.int32, (lanes, rows), 0)
    place = lax.broadcasted_iota(jnp.int32, (lanes, rows), 1)
    owner = lax.broadcasted_iota(jnp.int32, (heads, rows), 0)
    token = lax.broadcasted_iota(jnp.int32, (heads, rows), 1)
    high = sums.astype(BF16)
    rest = sums - high.astype(F32)
    mid = rest.astype(BF16)
    low = (rest - mid.astype(F32)).astype(BF16)
    terms = jnp.concatenate([high, mid, low], axis=0)
    pick = jnp.where(lane == place % n, 1.0, 0.0).astype(BF16)
    spread = dot_nn(terms, pick)
    spread = spread[0:heads] + spread[heads:2 * heads] + spread[2 * heads:]
    return jnp.sum(jnp.where(token // n == owner, spread, 0.0), axis=0, keepdims=True)


def split_scaled(x, e):
    y = x * jnp.exp2(14.0 - e)
    high = jnp.floor(y * (1.0 / 16.0)) * 16.0
    return high, y - high


def add_stats(s, scale, max_ref, sum_ref, ti, first):
    new = LOWEST if first else max_ref[ti, :]
    size = s.shape[1]
    for g in range(0, size, 128):
        new = jnp.maximum(new, s[:, g:g + 128])
    acc = 0.0 if first else sum_ref[ti, :] * jnp.exp2((max_ref[ti, :] - new) * scale)
    for g in range(0, size, 128):
        acc = acc + jnp.exp2((s[:, g:g + 128] - new) * scale)
    max_ref[ti, :] = new
    sum_ref[ti, :] = acc


def take(ref, at, n):
    heads, _, width = ref.shape
    return ref[:, at * n:(at + 1) * n, :].reshape(heads * n, width)


def pack_kernel(*refs):
    parts, steps_ref, out_ref = refs[:-2], refs[-2], refs[-1]
    n, heads, _ = parts[0].shape
    for at, ref in enumerate(parts):
        out_ref[:, at * n:(at + 1) * n, :] = jnp.swapaxes(ref[...], 0, 1)
    steps = jnp.concatenate([steps_ref[...].astype(F32), jnp.zeros((128 - n, heads), F32)], axis=0)
    last = len(parts) * n
    out_ref[:, last:last + 1, :] = jnp.transpose(steps).reshape(heads, 1, 128).astype(BF16)


def own_stats_kernel(n, scale, level_ref, own_ref, local_ref, max_ref, sum_ref):
    rows = max_ref.shape[0]
    heads = own_ref.shape[0]
    k, q = take(own_ref, 0, n), take(own_ref, 1, n)
    for at in range(0, rows, TILE):
        ti = slice(at, at + TILE)
        s = dot_nt(q[ti, :], k[0:at + TILE, :])
        row = lax.broadcasted_iota(jnp.int32, s.shape, 0) + at
        col = lax.broadcasted_iota(jnp.int32, s.shape, 1)
        add_stats(jnp.where(col <= row, s, LOWEST), scale, max_ref, sum_ref, ti, True)

    level = jnp.full((1, 1), level_ref[0], jnp.int32).astype(F32)
    steps = own_ref[:, 4 * n:4 * n + 1, :].astype(F32).reshape(heads, 128)
    local = sums_rows(-jnp.exp2(-0.5 * level) * steps, rows, n)
    local_ref[...] = jnp.broadcast_to(local, local_ref.shape)


def stats_kernel(
    n, scale, block_ref, own_ref, in1_ref, in2_ref, in3_ref, local_ref, max_ref, sum_ref,
    out_ref, score_ref, q_s, k_s, max_s, sum_s,
):
    block = block_ref[0]
    k_s[0, :, :] = take(own_ref, 0, n)
    rows = q_s.shape[0]
    q_s[...] = take(own_ref, 1, n)
    max_s[...] = max_ref[...]
    sum_s[...] = sum_ref[...]
    for d, in_ref in enumerate((in1_ref, in2_ref, in3_ref)):
        k_s[d + 1, :, :] = take(in_ref, 0, n)

    @pl.loop(1, block + 1)
    def _(d):
        s = dot_nt(q_s[...], k_s[d])
        score_ref[d - 1, :, :] = s
        add_stats(s, scale, max_s, sum_s, slice(None), False)

    @pl.loop(block + 1, 4)
    def _(d):
        score_ref[d - 1, :, :] = dot_nt(k_s[d], k_s[0])

    top = jnp.max(max_s[...], axis=1, keepdims=True)
    total = jnp.sum(sum_s[...] * jnp.exp2((max_s[...] - top) * scale), axis=1, keepdims=True)
    lane = lax.broadcasted_iota(jnp.int32, (rows, 8), 1)
    out_ref[...] = jnp.transpose(jnp.where(lane == 0, top, 1.0 / total))
    out_ref[2:3, :] = local_ref[0:1, :]


def fill_vec(block, stats_refs, vec_ref):
    local = [x[2:3, :] for x in stats_refs]
    rows = vec_ref.shape[1]
    ends = [x[:, rows - 1:rows] for x in local]
    vec_ref[0:1, :] = local[0]
    vec_ref[7:8, :] = jnp.zeros((1, rows), F32)
    for d in range(1, 4):
        nearer, farther = jnp.zeros((1, 1), F32), jnp.zeros((1, 1), F32)
        for g in range(1, d):
            nearer = nearer + ends[g]
        for g in range(d + 1, 4):
            farther = farther + ends[g]
        row_side = block >= d
        v = jnp.where(row_side, ends[d] - local[d], ends[0] - local[0])
        u = jnp.where(row_side, local[0] + nearer, local[d] + farther)
        vec_ref[d:d + 1, :] = jnp.exp2(v * LOG2E)
        vec_ref[3 + d:4 + d, :] = jnp.exp2(u * LOG2E)


def own_kernel(
    n, scale, beta, own_ref, stats_ref, gc_ref, gb_ref, sq_ref, gbt_s, cols_s,
):
    rows = gc_ref.shape[0]
    k_all, q_all, b_all, c_all = (take(own_ref, at, n) for at in range(4))
    ct = jnp.transpose(c_all.astype(F32)).astype(BF16)
    cols_s[...] = jnp.transpose(stats_ref[...])
    sq = jnp.zeros((8, 128), F32)
    gbt_s[...] = jnp.zeros(gbt_s.shape, F32)
    for i in range(0, rows, OWN):
        ti = slice(i, i + OWN)
        q, c = q_all[ti, :], c_all[ti, :]
        top_i, rinv_i, sum_i = cols_s[ti, 0:1], cols_s[ti, 1:2], cols_s[ti, 2:3]
        gc = 0.0
        for j in range(0, i + OWN, OWN):
            tj = slice(j, j + OWN)
            k, b = k_all[tj, :], b_all[tj, :]
            s = dot_nt(q, k) - top_i
            gap = sum_i - stats_ref[2:3, tj]
            if i == j:
                row = lax.broadcasted_iota(jnp.int32, s.shape, 0)
                col = lax.broadcasted_iota(jnp.int32, s.shape, 1)
                s = jnp.where(col <= row, s, LOWEST)
                gap = jnp.where(col <= row, gap, LOWEST)
            teacher = jnp.exp2(s * scale) * rinv_i
            decay = jnp.exp2(gap * LOG2E)
            error = (dot_nt(c, b) * beta) * decay - teacher
            sq = sq + fold_rows(error * error)
            held = (error * decay).astype(BF16)
            gc = gc + dot_nn(held, b)
            gbt_s[:, tj] += dot_nn(ct[:, ti], held)
        gc_ref[ti, :] = gc
    gb_ref[...] = jnp.transpose(gbt_s[...])
    sq_ref[...] = sq


def rows_kernel(
    n, scale, beta, block_ref, own_ref, b1_ref, b2_ref, b3_ref, score_ref,
    stats_ref, st1_ref, st2_ref, st3_ref, gc_in_ref, sq_in_ref, gc_ref, out_ref, vec_ref,
    c_s, b_s, cols_s, u_s, sq_s, cross_s,
):
    block = block_ref[0]
    rows, width = c_s.shape
    fill_vec(block, (stats_ref, st1_ref, st2_ref, st3_ref), vec_ref)
    c_s[...] = take(own_ref, 3, n)
    for d, b_ref in enumerate((b1_ref, b2_ref, b3_ref)):
        b_s[d + 1, :, :] = take(b_ref, 0, n)
    cols_s[...] = jnp.transpose(stats_ref[...])
    spread = jnp.transpose(vec_ref[...])
    for d in range(1, 4):
        u_s[d, :, :] = spread[:, 3 + d:4 + d]
    gc_ref[...] = gc_in_ref[...]
    sq_s[...] = sq_in_ref[...]
    cross_s[...] = jnp.zeros(cross_s.shape, F32)
    lane = lax.broadcasted_iota(jnp.int32, (1, 128), 1)

    @pl.loop(1, block + 1)
    def _(d):
        cross = jnp.zeros((1, 1), F32)
        sq = sq_s[...]
        for i in range(0, rows, TALL):
            ti = slice(i, i + TALL)
            held = []
            for j in range(0, rows, TILE):
                tj = slice(j, j + TILE)
                b = b_s[d, tj, :]
                teacher = jnp.exp2((score_ref[d - 1, ti, tj] - cols_s[ti, 0:1]) * scale)
                decay = u_s[d, ti, :] * vec_ref[pl.ds(d, 1), tj]
                error = (dot_nt(c_s[ti, :], b) * beta) * decay - teacher * cols_s[ti, 1:2]
                sq = sq + fold_rows(error * error)
                held.append((error * decay).astype(BF16))
            gc = dot_nn(jnp.concatenate(held, axis=1), b_s[d])
            cross = cross + total_of(gc * c_s[ti, :].astype(F32))
            gc_ref[ti, :] += gc
        cross_s[...] += jnp.where((lane < block) & (lane >= block - d), cross * beta, 0.0)
        sq_s[...] = sq

    sums = jnp.where(lane == 3, total_of(sq_s[...]), cross_s[...])
    out_ref[...] = jnp.broadcast_to(sums, out_ref.shape)


def cols_kernel(
    n, scale, beta, block_ref, own_ref, c1_ref, c2_ref, c3_ref, score_ref, vec_ref,
    st1_ref, st2_ref, st3_ref, gb_in_ref, sums_in_ref, gb_ref, sums_ref,
    b_s, c_s, cols_s, gbt_s,
):
    block = block_ref[0]
    rows, width = b_s.shape
    sums_ref[...] = sums_in_ref[...]
    b_s[...] = take(own_ref, 2, n)
    place = lax.broadcasted_iota(jnp.int32, (8, rows), 0)
    incoming = ((c1_ref, st1_ref), (c2_ref, st2_ref), (c3_ref, st3_ref))
    for d, (c_ref, st_ref) in enumerate(incoming):
        c_s[d + 1, :, :] = take(c_ref, 0, n)
        cols_s[d + 1, :, :] = jnp.transpose(
            jnp.where(place == 0, st_ref[0:1, :],
                      jnp.where(place == 1, st_ref[1:2, :], vec_ref[4 + d:5 + d, :]))
        )
    gbt_s[...] = jnp.zeros(gbt_s.shape, F32)

    @pl.loop(block + 1, 4)
    def _(d):
        c = c_s[d]
        ct = jnp.transpose(c.astype(F32)).astype(BF16)
        top_i, rinv_i, u_i = cols_s[d, :, 0:1], cols_s[d, :, 1:2], cols_s[d, :, 2:3]
        for j in range(0, rows, WIDE):
            tj = slice(j, j + WIDE)
            teacher = jnp.exp2((score_ref[d - 1, :, tj] - top_i) * scale) * rinv_i
            decay = u_i * vec_ref[pl.ds(d, 1), tj]
            error = (dot_nt(c, b_s[tj, :]) * beta) * decay - teacher
            gbt_s[:, tj] += dot_nn(ct, (error * decay).astype(BF16))

    gb_ref[...] = gb_in_ref[...] + jnp.transpose(gbt_s[...])


def finish_kernel(
    n, beta, seq_len, block_ref, level_ref, own_ref, gc_ref, gb_ref,
    sums0_ref, sums1_ref, sums2_ref, sums3_ref, out_ref,
):
    block = block_ref[0]
    heads, _, width = own_ref.shape
    rows = heads * n
    gb = gb_ref[...]
    gc = gc_ref[...]
    c = take(own_ref, 3, n).astype(F32)
    b = take(own_ref, 2, n).astype(F32)
    slope = jnp.sum(c * gc - b * gb, axis=1, keepdims=True) * beta
    slope = jnp.broadcast_to(slope, (rows, 128)).reshape(heads, n, 128)
    place = lax.broadcasted_iota(jnp.int32, (heads, n, 128), 1)
    lane3 = lax.broadcasted_iota(jnp.int32, (heads, n, 128), 2)
    slope = jnp.sum(jnp.where(place == lane3 % n, slope, 0.0), axis=1)
    up = lax.broadcasted_iota(jnp.int32, (128, 128), 0)
    across = lax.broadcasted_iota(jnp.int32, (128, 128), 1)
    same = up // n == across // n
    inside = dot_full(slope, jnp.where(same & (up >= across), 1.0, 0.0).astype(F32))
    whole = dot_full(slope, jnp.where(same, 1.0, 0.0).astype(F32))
    down = lax.broadcasted_iota(jnp.int32, (heads, heads), 0)
    right = lax.broadcasted_iota(jnp.int32, (heads, heads), 1)
    behind = dot_full(jnp.where(right > down, 1.0, 0.0).astype(F32), whole)
    lane1 = lax.broadcasted_iota(jnp.int32, (1, 128), 1)
    sums = (sums0_ref[0:1, :] + sums1_ref[0:1, :]) + (sums2_ref[0:1, :] + sums3_ref[0:1, :])
    after = jnp.sum(
        jnp.where(jnp.logical_and(lane1 == block, block < 3), sums, 0.0), axis=1, keepdims=True
    )
    error_sq = jnp.sum(jnp.where(lane1 == 3, sums, 0.0), axis=1, keepdims=True)
    norm = jnp.sqrt(error_sq + 1e-06)
    factor = seq_len / norm
    rate = jnp.exp2(-0.5 * jnp.full((1, 1), level_ref[0], jnp.int32).astype(F32))
    step = (inside + behind + after) * (-(rate * factor))
    lane = lax.broadcasted_iota(jnp.int32, (heads, 128), 1)
    gb = gb * (factor * beta)
    gc = gc * (factor * beta)
    eb, ec, es, en = exponent_of(gb), exponent_of(gc), exponent_of(step), exponent_of(norm)
    out_ref[:, 0:n, :] = (gb * jnp.exp2(14.0 - eb)).reshape(heads, n, width)
    out_ref[:, n:2 * n, :] = (gc * jnp.exp2(14.0 - ec)).reshape(heads, n, width)
    high, low = split_scaled(step, es)
    norm_high, norm_low = split_scaled(norm, en)
    last = jnp.where(lane < n, high, low)
    for at, value in enumerate((eb, ec, es, norm_high, norm_low, en)):
        last = jnp.where(lane == 2 * n + at, value, last)
    out_ref[:, 2 * n:2 * n + 1, :] = last.reshape(heads, 1, 128)


def unpack_kernel(x_ref, gb_ref, gc_ref, step_ref, loss_ref):
    heads = x_ref.shape[0]
    n = gb_ref.shape[0]
    last = x_ref[:, 2 * n:2 * n + 1, :].reshape(heads, 128)
    lane = lax.broadcasted_iota(jnp.int32, (heads, 128), 1)

    def pick(at):
        return jnp.sum(jnp.where(lane == 2 * n + at, last, 0.0), axis=1, keepdims=True)

    scale_b, scale_c, scale_s = (jnp.exp2(pick(at) - 14.0) for at in range(3))
    norm = (pick(3) + pick(4)) * jnp.exp2(pick(5) - 14.0)
    gb_ref[...] = jnp.swapaxes(x_ref[:, 0:n, :] * scale_b[:, :, None], 0, 1)
    gc_ref[...] = jnp.swapaxes(x_ref[:, n:2 * n, :] * scale_c[:, :, None], 0, 1)
    step = jnp.transpose(last * scale_s)
    step_ref[...] = step[0:n, :] + step[n:2 * n, :]
    loss_ref[...] = jnp.sum(norm, axis=0, keepdims=True) * (1.0 / heads)


def call(kernel, out_shape, scratch, scalars, count):
    return pl.pallas_call(
        kernel,
        out_shape=out_shape,
        in_specs=[pl.BlockSpec(memory_space=pltpu.SMEM)] * scalars
        + [pl.BlockSpec(memory_space=pltpu.VMEM)] * (count - scalars),
        out_specs=jax.tree.map(lambda _: pl.BlockSpec(memory_space=pltpu.VMEM), out_shape),
        scratch_shapes=scratch,
        compiler_params=pltpu.CompilerParams(vmem_limit_bytes=VMEM_BYTES),
    )


def shape(*dims, dtype=F32):
    return jax.ShapeDtypeStruct(dims, dtype)


def near(*dims, dtype=F32):
    return pltpu.VMEM(dims, dtype)


def held_near(x):
    return pltpu.with_memory_space_constraint(x, pltpu.VMEM)


def per_device(queries, keys, b_proj, c_proj, step_size, rate_level):
    n, heads, width = queries.shape
    blocks = lax.axis_size("seq")
    block = lax.axis_index("seq")
    rows = n * heads
    seq_len = rows * blocks
    beta = 2.0 / math.sqrt(width * seq_len)
    scale = LOG2E / math.sqrt(width)

    def to_heads(x):
        return lax.all_to_all(x, "head", split_axis=0, concat_axis=0, tiled=True)

    def around(x):
        return [
            lax.ppermute(x, "seq", [(i, (i + d) % blocks) for i in range(blocks)])
            for d in range(1, blocks)
        ]

    def exchange(pair, ahead=None):
        mine, after = pair[:, 0:n], pair[:, n:2 * n]
        out = []
        for d in range(1, blocks):
            sent = jnp.where(block + d < blocks, mine, after)
            if ahead is not None and d == 1:
                sent, ahead[2] = lax.optimization_barrier((sent, ahead[2]))
            out.append(
                lax.ppermute(sent, "seq", [(i, (i + d) % blocks) for i in range(blocks)])
            )
        return out

    inputs = [
        pltpu.with_memory_space_constraint(x, pltpu.HBM)
        for x in (keys, queries, b_proj, c_proj, step_size)
    ]
    arrived = to_heads(
        call(pack_kernel, near(heads, 4 * n + 1, width, dtype=BF16), [], 0, 5)(*inputs)
    )
    kq_from = exchange(arrived[:, 0:2 * n])
    own = held_near(arrived)
    where = jnp.reshape(block, (1,)).astype(jnp.int32)
    mat = pltpu.VMEM((rows, width), BF16)
    mats = pltpu.VMEM((blocks, rows, width), BF16)
    flat = pltpu.VMEM((width, rows), F32)
    state = pltpu.VMEM((rows, 128), F32)
    local, top, total = call(
        functools.partial(own_stats_kernel, n, scale),
        [near(8, rows), near(rows, 128), near(rows, 128)], [], 1, 2,
    )(rate_level, own)
    bc, local = lax.optimization_barrier((arrived[:, 2 * n:4 * n], local))
    bc_from = exchange(bc, kq_from)
    kq_from, bc_from = [[held_near(x) for x in y] for y in (kq_from, bc_from)]
    stats, scores = call(
        functools.partial(stats_kernel, n, scale),
        [near(8, rows), near(blocks - 1, rows, rows)], [mat, mats, state, state], 1, 8,
    )(where, own, *kq_from, local, top, total)
    stats_from = [held_near(x) for x in around(stats)]
    gc, gb, sq = call(
        functools.partial(own_kernel, n, scale, beta),
        [near(rows, width), near(rows, width), near(8, 128)],
        [flat, pltpu.VMEM((rows, 8), F32)], 0, 2,
    )(own, stats)
    gc, sums, vec = call(
        functools.partial(rows_kernel, n, scale, beta),
        [near(rows, width), near(8, 128), near(8, rows)],
        [
            mat, mats, pltpu.VMEM((rows, 8), F32),
            pltpu.VMEM((4, rows, 1), F32), pltpu.VMEM((8, 128), F32), pltpu.VMEM((1, 128), F32),
        ],
        1, 12,
    )(where, own, *bc_from, scores, stats, *stats_from, gc, sq)
    gb, sums = call(
        functools.partial(cols_kernel, n, scale, beta),
        [near(rows, width), near(8, 128)],
        [mat, mats, pltpu.VMEM((4, rows, 8), F32), flat],
        1, 12,
    )(where, own, *bc_from, scores, vec, *stats_from, gb, sums)
    sums_from = [held_near(x) for x in around(sums)]
    packed = call(
        functools.partial(finish_kernel, n, beta, float(seq_len)),
        near(heads, 2 * n + 1, width), [], 2, 9,
    )(where, rate_level, own, gc, gb, sums, *sums_from)
    back = to_heads(packed.astype(F16)).astype(F32)
    grad_b, grad_c, grad_step, loss = pl.pallas_call(
        unpack_kernel,
        out_shape=[
            shape(n, heads, width), shape(n, heads, width), shape(n, heads), shape(1, 1),
        ],
        compiler_params=pltpu.CompilerParams(vmem_limit_bytes=VMEM_BYTES),
    )(held_near(back))
    return grad_b, grad_c, grad_step, jnp.reshape(loss, ())


def solution(mesh):
    tokens = P(("seq", "head"), None, None)
    return jax.shard_map(
        per_device,
        mesh=mesh,
        in_specs=(tokens, tokens, tokens, tokens, P(("seq", "head"), None), P("head")),
        out_specs=(tokens, tokens, P(("seq", "head"), None), P()),
        check_vma=False,
    )
```

```python
import functools
import math

import jax
import jax.numpy as jnp
from jax import lax
from jax.experimental import pallas as pl
from jax.experimental.pallas import tpu as pltpu
from jax.sharding import PartitionSpec as P

F32 = jnp.float32
BF16 = jnp.bfloat16
F16 = jnp.float16
LOG2E = math.log2(math.e)
TILE = 256
TALL = 512
WIDE = 512
OWN = 512
LOWEST = -1e30
VMEM_BYTES = 32 * 1024 * 1024


def dot_nt(a, b):
    return lax.dot_general(a, b, (((1,), (1,)), ((), ())), preferred_element_type=F32)


def dot_nn(a, b):
    return lax.dot_general(a, b, (((1,), (0,)), ((), ())), preferred_element_type=F32)


def dot_full(a, b):
    return lax.dot_general(
        a, b, (((1,), (0,)), ((), ())),
        precision=lax.Precision.HIGHEST, preferred_element_type=F32,
    )


def fold_rows(x):
    rows, cols = x.shape
    x = jnp.sum(x.reshape(rows // 8, 8, cols), axis=0)
    out = x[:, :128]
    for at in range(128, cols, 128):
        out = out + x[:, at:at + 128]
    return out


def total_of(x):
    return jnp.sum(jnp.sum(x, axis=0, keepdims=True), axis=1, keepdims=True)


def exponent_of(x):
    top = jnp.max(jnp.max(jnp.abs(x), axis=0, keepdims=True), axis=1, keepdims=True)
    return jnp.floor(jnp.log2(jnp.maximum(top, 1e-30)))


def sums_rows(log_decay, rows, n):
    heads, lanes = log_decay.shape
    up = lax.broadcasted_iota(jnp.int32, (lanes, lanes), 0)
    across = lax.broadcasted_iota(jnp.int32, (lanes, lanes), 1)
    same = up // n == across // n
    inside = dot_full(log_decay, jnp.where(same & (up <= across), 1.0, 0.0).astype(F32))
    whole = dot_full(log_decay, jnp.where(same, 1.0, 0.0).astype(F32))
    down = lax.broadcasted_iota(jnp.int32, (heads, heads), 0)
    right = lax.broadcasted_iota(jnp.int32, (heads, heads), 1)
    sums = inside + dot_full(jnp.where(right < down, 1.0, 0.0).astype(F32), whole)
    lane = lax.broadcasted_iota(jnp.int32, (lanes, rows), 0)
    place = lax.broadcasted_iota(jnp.int32, (lanes, rows), 1)
    owner = lax.broadcasted_iota(jnp.int32, (heads, rows), 0)
    token = lax.broadcasted_iota(jnp.int32, (heads, rows), 1)
    high = sums.astype(BF16)
    rest = sums - high.astype(F32)
    mid = rest.astype(BF16)
    low = (rest - mid.astype(F32)).astype(BF16)
    terms = jnp.concatenate([high, mid, low], axis=0)
    pick = jnp.where(lane == place % n, 1.0, 0.0).astype(BF16)
    spread = dot_nn(terms, pick)
    spread = spread[0:heads] + spread[heads:2 * heads] + spread[2 * heads:]
    return jnp.sum(jnp.where(token // n == owner, spread, 0.0), axis=0, keepdims=True)


def split_scaled(x, e):
    y = x * jnp.exp2(14.0 - e)
    high = jnp.floor(y * (1.0 / 16.0)) * 16.0
    return high, y - high


def add_stats(s, max_ref, sum_ref, ti, first):
    new = LOWEST if first else max_ref[ti, :]
    size = s.shape[1]
    for g in range(0, size, 128):
        new = jnp.maximum(new, s[:, g:g + 128])
    acc = 0.0 if first else sum_ref[ti, :] * jnp.exp2(max_ref[ti, :] - new)
    for g in range(0, size, 128):
        acc = acc + jnp.exp2(s[:, g:g + 128] - new)
    max_ref[ti, :] = new
    sum_ref[ti, :] = acc


def take(ref, at, n):
    heads, _, width = ref.shape
    return ref[:, at * n:(at + 1) * n, :].reshape(heads * n, width)


def pack_kernel(*refs):
    parts, steps_ref, out_ref = refs[:-2], refs[-2], refs[-1]
    n, heads, _ = parts[0].shape
    for at, ref in enumerate(parts):
        out_ref[:, at * n:(at + 1) * n, :] = jnp.swapaxes(ref[...], 0, 1)
    steps = jnp.concatenate([steps_ref[...].astype(F32), jnp.zeros((128 - n, heads), F32)], axis=0)
    last = len(parts) * n
    out_ref[:, last:last + 1, :] = jnp.transpose(steps).reshape(heads, 1, 128).astype(BF16)


def own_stats_kernel(n, scale, level_ref, own_ref, local_ref, max_ref, sum_ref):
    rows = max_ref.shape[0]
    heads = own_ref.shape[0]
    k, q = take(own_ref, 0, n), take(own_ref, 1, n)
    for at in range(0, rows, TILE):
        ti = slice(at, at + TILE)
        s = dot_nt(q[ti, :], k[0:at + TILE, :]) * scale
        row = lax.broadcasted_iota(jnp.int32, s.shape, 0) + at
        col = lax.broadcasted_iota(jnp.int32, s.shape, 1)
        add_stats(jnp.where(col <= row, s, LOWEST), max_ref, sum_ref, ti, True)

    level = jnp.full((1, 1), level_ref[0], jnp.int32).astype(F32)
    steps = own_ref[:, 4 * n:4 * n + 1, :].astype(F32).reshape(heads, 128)
    local = sums_rows(-jnp.exp2(-0.5 * level) * steps, rows, n)
    local_ref[...] = jnp.broadcast_to(local, local_ref.shape)


def stats_kernel(
    n, scale, block_ref, own_ref, in1_ref, in2_ref, in3_ref, local_ref, max_ref, sum_ref,
    out_ref, score_ref, q_s, k_s, max_s, sum_s,
):
    block = block_ref[0]
    k_s[0, :, :] = take(own_ref, 0, n)
    rows = q_s.shape[0]
    q_s[...] = take(own_ref, 1, n)
    max_s[...] = max_ref[...]
    sum_s[...] = sum_ref[...]
    for d, in_ref in enumerate((in1_ref, in2_ref, in3_ref)):
        k_s[d + 1, :, :] = take(in_ref, 0, n)

    @pl.loop(1, block + 1)
    def _(d):
        s = dot_nt(q_s[...], k_s[d]) * scale
        score_ref[d - 1, :, :] = s
        add_stats(s, max_s, sum_s, slice(None), False)

    @pl.loop(block + 1, 4)
    def _(d):
        score_ref[d - 1, :, :] = dot_nt(k_s[d], k_s[0]) * scale

    top = jnp.max(max_s[...], axis=1, keepdims=True)
    total = jnp.sum(sum_s[...] * jnp.exp2(max_s[...] - top), axis=1, keepdims=True)
    out_ref[...] = jnp.transpose(jnp.broadcast_to(top + jnp.log2(total), (rows, 8)))
    out_ref[2:3, :] = local_ref[0:1, :]


def fill_vec(block, stats_refs, vec_ref):
    local = [x[2:3, :] for x in stats_refs]
    rows = vec_ref.shape[1]
    ends = [x[:, rows - 1:rows] for x in local]
    vec_ref[0:1, :] = local[0]
    vec_ref[7:8, :] = jnp.zeros((1, rows), F32)
    for d in range(1, 4):
        nearer, farther = jnp.zeros((1, 1), F32), jnp.zeros((1, 1), F32)
        for g in range(1, d):
            nearer = nearer + ends[g]
        for g in range(d + 1, 4):
            farther = farther + ends[g]
        row_side = block >= d
        v = jnp.where(row_side, ends[d] - local[d], ends[0] - local[0])
        u = jnp.where(row_side, local[0] + nearer, local[d] + farther)
        vec_ref[d:d + 1, :] = jnp.exp2(v * LOG2E)
        vec_ref[3 + d:4 + d, :] = jnp.exp2(u * LOG2E)


def own_kernel(
    n, scale, beta, own_ref, stats_ref, gc_ref, gb_ref, sq_ref, gbt_s, cols_s,
):
    rows = gc_ref.shape[0]
    k_all, q_all, b_all, c_all = (take(own_ref, at, n) for at in range(4))
    ct = jnp.transpose(c_all.astype(F32)).astype(BF16)
    cols_s[...] = jnp.transpose(stats_ref[...])
    sq = jnp.zeros((8, 128), F32)
    gbt_s[...] = jnp.zeros(gbt_s.shape, F32)
    for i in range(0, rows, OWN):
        ti = slice(i, i + OWN)
        q, c = q_all[ti, :], c_all[ti, :]
        top_i, sum_i = cols_s[ti, 0:1], cols_s[ti, 2:3]
        gc = 0.0
        for j in range(0, i + OWN, OWN):
            tj = slice(j, j + OWN)
            k, b = k_all[tj, :], b_all[tj, :]
            s = dot_nt(q, k) * scale - top_i
            gap = sum_i - stats_ref[2:3, tj]
            if i == j:
                row = lax.broadcasted_iota(jnp.int32, s.shape, 0)
                col = lax.broadcasted_iota(jnp.int32, s.shape, 1)
                s = jnp.where(col <= row, s, LOWEST)
                gap = jnp.where(col <= row, gap, LOWEST)
            teacher = jnp.exp2(s)
            decay = jnp.exp2(gap * LOG2E)
            error = (dot_nt(c, b) * beta) * decay - teacher
            sq = sq + fold_rows(error * error)
            held = (error * decay).astype(BF16)
            gc = gc + dot_nn(held, b)
            gbt_s[:, tj] += dot_nn(ct[:, ti], held)
        gc_ref[ti, :] = gc
    gb_ref[...] = jnp.transpose(gbt_s[...])
    sq_ref[...] = sq


def blocks_kernel(
    n, beta, block_ref, own_ref, in1_ref, in2_ref, in3_ref, score_ref,
    stats_ref, st1_ref, st2_ref, st3_ref, gc_in_ref, gb_in_ref, sq_in_ref,
    gc_ref, gb_ref, out_ref,
    b_s, c_s, in_s, vec_s, cols_s, gbt_s, sq_s, cross_s,
):
    block = block_ref[0]
    rows, width = c_s.shape
    b_s[...] = take(own_ref, 2, n)
    c_s[...] = take(own_ref, 3, n)
    fill_vec(block, (stats_ref, st1_ref, st2_ref, st3_ref), vec_s)
    place = lax.broadcasted_iota(jnp.int32, (8, rows), 0)
    incoming = ((in1_ref, st1_ref), (in2_ref, st2_ref), (in3_ref, st3_ref))
    for d, (in_ref, st_ref) in enumerate(incoming, 1):
        in_s[d, :, :] = take(in_ref, 0, n)
        top = jnp.where(block >= d, stats_ref[0:1, :], st_ref[0:1, :])
        cols_s[d, :, :] = jnp.transpose(jnp.where(place == 0, top, vec_s[3 + d:4 + d, :]))
    gc_ref[...] = gc_in_ref[...]
    sq_s[...] = sq_in_ref[...]
    cross_s[...] = jnp.zeros(cross_s.shape, F32)
    gbt_s[...] = jnp.zeros(gbt_s.shape, F32)
    lane = lax.broadcasted_iota(jnp.int32, (1, 128), 1)

    @pl.loop(1, block + 1)
    def _(d):
        cross = jnp.zeros((1, 1), F32)
        sq = sq_s[...]
        for i in range(0, rows, TALL):
            ti = slice(i, i + TALL)
            held = []
            for j in range(0, rows, TILE):
                tj = slice(j, j + TILE)
                teacher = jnp.exp2(score_ref[d - 1, ti, tj] - cols_s[d, ti, 0:1])
                decay = cols_s[d, ti, 1:2] * vec_s[pl.ds(d, 1), tj]
                error = (dot_nt(c_s[ti, :], in_s[d, tj, :]) * beta) * decay - teacher
                sq = sq + fold_rows(error * error)
                held.append((error * decay).astype(BF16))
            gc = dot_nn(jnp.concatenate(held, axis=1), in_s[d])
            cross = cross + total_of(gc * c_s[ti, :].astype(F32))
            gc_ref[ti, :] += gc
        cross_s[...] += jnp.where((lane < block) & (lane >= block - d), cross * beta, 0.0)
        sq_s[...] = sq

    @pl.loop(block + 1, 4)
    def _(d):
        c = in_s[d]
        ct = jnp.transpose(c.astype(F32)).astype(BF16)
        top_i, u_i = cols_s[d, :, 0:1], cols_s[d, :, 1:2]
        for j in range(0, rows, WIDE):
            tj = slice(j, j + WIDE)
            teacher = jnp.exp2(score_ref[d - 1, :, tj] - top_i)
            decay = u_i * vec_s[pl.ds(d, 1), tj]
            error = (dot_nt(c, b_s[tj, :]) * beta) * decay - teacher
            gbt_s[:, tj] += dot_nn(ct, (error * decay).astype(BF16))

    gb_ref[...] = gb_in_ref[...] + jnp.transpose(gbt_s[...])
    sums = jnp.where(lane == 3, total_of(sq_s[...]), cross_s[...])
    out_ref[...] = jnp.broadcast_to(sums, out_ref.shape)


def finish_kernel(
    n, beta, seq_len, block_ref, level_ref, own_ref, gc_ref, gb_ref,
    sums0_ref, sums1_ref, sums2_ref, sums3_ref, out_ref,
):
    block = block_ref[0]
    heads, _, width = own_ref.shape
    rows = heads * n
    gb = gb_ref[...]
    gc = gc_ref[...]
    c = take(own_ref, 3, n).astype(F32)
    b = take(own_ref, 2, n).astype(F32)
    slope = jnp.sum(c * gc - b * gb, axis=1, keepdims=True) * beta
    slope = jnp.broadcast_to(slope, (rows, 128)).reshape(heads, n, 128)
    place = lax.broadcasted_iota(jnp.int32, (heads, n, 128), 1)
    lane3 = lax.broadcasted_iota(jnp.int32, (heads, n, 128), 2)
    slope = jnp.sum(jnp.where(place == lane3 % n, slope, 0.0), axis=1)
    up = lax.broadcasted_iota(jnp.int32, (128, 128), 0)
    across = lax.broadcasted_iota(jnp.int32, (128, 128), 1)
    same = up // n == across // n
    inside = dot_full(slope, jnp.where(same & (up >= across), 1.0, 0.0).astype(F32))
    whole = dot_full(slope, jnp.where(same, 1.0, 0.0).astype(F32))
    down = lax.broadcasted_iota(jnp.int32, (heads, heads), 0)
    right = lax.broadcasted_iota(jnp.int32, (heads, heads), 1)
    behind = dot_full(jnp.where(right > down, 1.0, 0.0).astype(F32), whole)
    lane1 = lax.broadcasted_iota(jnp.int32, (1, 128), 1)
    sums = (sums0_ref[0:1, :] + sums1_ref[0:1, :]) + (sums2_ref[0:1, :] + sums3_ref[0:1, :])
    after = jnp.sum(
        jnp.where(jnp.logical_and(lane1 == block, block < 3), sums, 0.0), axis=1, keepdims=True
    )
    error_sq = jnp.sum(jnp.where(lane1 == 3, sums, 0.0), axis=1, keepdims=True)
    norm = jnp.sqrt(error_sq + 1e-06)
    factor = seq_len / norm
    rate = jnp.exp2(-0.5 * jnp.full((1, 1), level_ref[0], jnp.int32).astype(F32))
    step = (inside + behind + after) * (-(rate * factor))
    lane = lax.broadcasted_iota(jnp.int32, (heads, 128), 1)
    gb = gb * (factor * beta)
    gc = gc * (factor * beta)
    eb, ec, es, en = exponent_of(gb), exponent_of(gc), exponent_of(step), exponent_of(norm)
    out_ref[:, 0:n, :] = (gb * jnp.exp2(14.0 - eb)).reshape(heads, n, width)
    out_ref[:, n:2 * n, :] = (gc * jnp.exp2(14.0 - ec)).reshape(heads, n, width)
    high, low = split_scaled(step, es)
    norm_high, norm_low = split_scaled(norm, en)
    last = jnp.where(lane < n, high, low)
    for at, value in enumerate((eb, ec, es, norm_high, norm_low, en)):
        last = jnp.where(lane == 2 * n + at, value, last)
    out_ref[:, 2 * n:2 * n + 1, :] = last.reshape(heads, 1, 128)


def unpack_kernel(x_ref, gb_ref, gc_ref, step_ref, loss_ref):
    heads = x_ref.shape[0]
    n = gb_ref.shape[0]
    last = x_ref[:, 2 * n:2 * n + 1, :].reshape(heads, 128)
    lane = lax.broadcasted_iota(jnp.int32, (heads, 128), 1)

    def pick(at):
        return jnp.sum(jnp.where(lane == 2 * n + at, last, 0.0), axis=1, keepdims=True)

    scale_b, scale_c, scale_s = (jnp.exp2(pick(at) - 14.0) for at in range(3))
    norm = (pick(3) + pick(4)) * jnp.exp2(pick(5) - 14.0)
    gb_ref[...] = jnp.swapaxes(x_ref[:, 0:n, :] * scale_b[:, :, None], 0, 1)
    gc_ref[...] = jnp.swapaxes(x_ref[:, n:2 * n, :] * scale_c[:, :, None], 0, 1)
    step = jnp.transpose(last * scale_s)
    step_ref[...] = step[0:n, :] + step[n:2 * n, :]
    loss_ref[...] = jnp.sum(norm, axis=0, keepdims=True) * (1.0 / heads)


def call(kernel, out_shape, scratch, scalars, count):
    return pl.pallas_call(
        kernel,
        out_shape=out_shape,
        in_specs=[pl.BlockSpec(memory_space=pltpu.SMEM)] * scalars
        + [pl.BlockSpec(memory_space=pltpu.VMEM)] * (count - scalars),
        out_specs=jax.tree.map(lambda _: pl.BlockSpec(memory_space=pltpu.VMEM), out_shape),
        scratch_shapes=scratch,
        compiler_params=pltpu.CompilerParams(vmem_limit_bytes=VMEM_BYTES),
    )


def shape(*dims, dtype=F32):
    return jax.ShapeDtypeStruct(dims, dtype)


def near(*dims, dtype=F32):
    return pltpu.VMEM(dims, dtype)


def held_near(x):
    return pltpu.with_memory_space_constraint(x, pltpu.VMEM)


def per_device(queries, keys, b_proj, c_proj, step_size, rate_level):
    n, heads, width = queries.shape
    blocks = lax.axis_size("seq")
    block = lax.axis_index("seq")
    rows = n * heads
    seq_len = rows * blocks
    beta = 2.0 / math.sqrt(width * seq_len)
    scale = LOG2E / math.sqrt(width)

    def to_heads(x):
        return lax.all_to_all(x, "head", split_axis=0, concat_axis=0, tiled=True)

    def around(x):
        return [
            lax.ppermute(x, "seq", [(i, (i + d) % blocks) for i in range(blocks)])
            for d in range(1, blocks)
        ]

    def exchange(pair, ahead=None):
        mine, after = pair[:, 0:n], pair[:, n:2 * n]
        out = []
        for d in range(1, blocks):
            sent = jnp.where(block + d < blocks, mine, after)
            if ahead is not None and d == 1:
                sent, ahead[2] = lax.optimization_barrier((sent, ahead[2]))
            out.append(
                lax.ppermute(sent, "seq", [(i, (i + d) % blocks) for i in range(blocks)])
            )
        return out

    inputs = [
        pltpu.with_memory_space_constraint(x, pltpu.HBM)
        for x in (keys, queries, b_proj, c_proj, step_size)
    ]
    arrived = to_heads(
        call(pack_kernel, near(heads, 4 * n + 1, width, dtype=BF16), [], 0, 5)(*inputs)
    )
    kq_from = exchange(arrived[:, 0:2 * n])
    own = held_near(arrived)
    where = jnp.reshape(block, (1,)).astype(jnp.int32)
    mat = pltpu.VMEM((rows, width), BF16)
    mats = pltpu.VMEM((blocks, rows, width), BF16)
    flat = pltpu.VMEM((width, rows), F32)
    state = pltpu.VMEM((rows, 128), F32)
    local, top, total = call(
        functools.partial(own_stats_kernel, n, scale),
        [near(8, rows), near(rows, 128), near(rows, 128)], [], 1, 2,
    )(rate_level, own)
    bc, local = lax.optimization_barrier((arrived[:, 2 * n:4 * n], local))
    bc_from = exchange(bc, kq_from)
    kq_from, bc_from = [[held_near(x) for x in y] for y in (kq_from, bc_from)]
    stats, scores = call(
        functools.partial(stats_kernel, n, scale),
        [near(8, rows), near(blocks - 1, rows, rows)], [mat, mats, state, state], 1, 8,
    )(where, own, *kq_from, local, top, total)
    stats_from = [held_near(x) for x in around(stats)]
    gc, gb, sq = call(
        functools.partial(own_kernel, n, scale, beta),
        [near(rows, width), near(rows, width), near(8, 128)],
        [flat, pltpu.VMEM((rows, 8), F32)], 0, 2,
    )(own, stats)
    gc, gb, sums = call(
        functools.partial(blocks_kernel, n, beta),
        [near(rows, width), near(rows, width), near(8, 128)],
        [
            mat, mat, mats, pltpu.VMEM((8, rows), F32), pltpu.VMEM((4, rows, 8), F32), flat,
            pltpu.VMEM((8, 128), F32), pltpu.VMEM((1, 128), F32),
        ],
        1, 13,
    )(where, own, *bc_from, scores, stats, *stats_from, gc, gb, sq)
    sums_from = [held_near(x) for x in around(sums)]
    packed = call(
        functools.partial(finish_kernel, n, beta, float(seq_len)),
        near(heads, 2 * n + 1, width), [], 2, 9,
    )(where, rate_level, own, gc, gb, sums, *sums_from)
    back = to_heads(packed.astype(F16)).astype(F32)
    grad_b, grad_c, grad_step, loss = pl.pallas_call(
        unpack_kernel,
        out_shape=[
            shape(n, heads, width), shape(n, heads, width), shape(n, heads), shape(1, 1),
        ],
        compiler_params=pltpu.CompilerParams(vmem_limit_bytes=VMEM_BYTES),
    )(held_near(back))
    return grad_b, grad_c, grad_step, jnp.reshape(loss, ())


def solution(mesh):
    tokens = P(("seq", "head"), None, None)
    return jax.shard_map(
        per_device,
        mesh=mesh,
        in_specs=(tokens, tokens, tokens, tokens, P(("seq", "head"), None), P("head")),
        out_specs=(tokens, tokens, P(("seq", "head"), None), P()),
        check_vma=False,
    )
```

```python
import functools
import math

import jax
import jax.numpy as jnp
from jax import lax
from jax.experimental import pallas as pl
from jax.experimental.pallas import tpu as pltpu
from jax.sharding import PartitionSpec as P

F32 = jnp.float32
BF16 = jnp.bfloat16
F16 = jnp.float16
LOG2E = math.log2(math.e)
TILE = 256
TALL = 512
WIDE = 512
OWN = 512
LOWEST = -1e30
VMEM_BYTES = 32 * 1024 * 1024


def dot_nt(a, b):
    return lax.dot_general(a, b, (((1,), (1,)), ((), ())), preferred_element_type=F32)


def dot_nn(a, b):
    return lax.dot_general(a, b, (((1,), (0,)), ((), ())), preferred_element_type=F32)


def dot_full(a, b):
    return lax.dot_general(
        a, b, (((1,), (0,)), ((), ())),
        precision=lax.Precision.HIGHEST, preferred_element_type=F32,
    )


def fold_rows(x):
    rows, cols = x.shape
    x = jnp.sum(x.reshape(rows // 8, 8, cols), axis=0)
    out = x[:, :128]
    for at in range(128, cols, 128):
        out = out + x[:, at:at + 128]
    return out


def total_of(x):
    return jnp.sum(jnp.sum(x, axis=0, keepdims=True), axis=1, keepdims=True)


def exponent_of(x):
    top = jnp.max(jnp.max(jnp.abs(x), axis=0, keepdims=True), axis=1, keepdims=True)
    return jnp.floor(jnp.log2(jnp.maximum(top, 1e-30)))


def sums_rows(log_decay, rows, n):
    heads, lanes = log_decay.shape
    up = lax.broadcasted_iota(jnp.int32, (lanes, lanes), 0)
    across = lax.broadcasted_iota(jnp.int32, (lanes, lanes), 1)
    same = up // n == across // n
    inside = dot_full(log_decay, jnp.where(same & (up <= across), 1.0, 0.0).astype(F32))
    whole = dot_full(log_decay, jnp.where(same, 1.0, 0.0).astype(F32))
    down = lax.broadcasted_iota(jnp.int32, (heads, heads), 0)
    right = lax.broadcasted_iota(jnp.int32, (heads, heads), 1)
    sums = inside + dot_full(jnp.where(right < down, 1.0, 0.0).astype(F32), whole)
    lane = lax.broadcasted_iota(jnp.int32, (lanes, rows), 0)
    place = lax.broadcasted_iota(jnp.int32, (lanes, rows), 1)
    owner = lax.broadcasted_iota(jnp.int32, (heads, rows), 0)
    token = lax.broadcasted_iota(jnp.int32, (heads, rows), 1)
    high = sums.astype(BF16)
    rest = sums - high.astype(F32)
    mid = rest.astype(BF16)
    low = (rest - mid.astype(F32)).astype(BF16)
    terms = jnp.concatenate([high, mid, low], axis=0)
    pick = jnp.where(lane == place % n, 1.0, 0.0).astype(BF16)
    spread = dot_nn(terms, pick)
    spread = spread[0:heads] + spread[heads:2 * heads] + spread[2 * heads:]
    return jnp.sum(jnp.where(token // n == owner, spread, 0.0), axis=0, keepdims=True)


def split_scaled(x, e):
    y = x * jnp.exp2(14.0 - e)
    high = jnp.floor(y * (1.0 / 16.0)) * 16.0
    return high, y - high


def add_stats(s, max_ref, sum_ref, ti, first):
    new = LOWEST if first else max_ref[ti, :]
    size = s.shape[1]
    for g in range(0, size, 128):
        new = jnp.maximum(new, s[:, g:g + 128])
    acc = 0.0 if first else sum_ref[ti, :] * jnp.exp2(max_ref[ti, :] - new)
    for g in range(0, size, 128):
        acc = acc + jnp.exp2(s[:, g:g + 128] - new)
    max_ref[ti, :] = new
    sum_ref[ti, :] = acc


def take(ref, at, n):
    heads, _, width = ref.shape
    return ref[:, at * n:(at + 1) * n, :].reshape(heads * n, width)


def pack_kernel(*refs):
    parts, steps_ref, out_ref = refs[:-2], refs[-2], refs[-1]
    n, heads, _ = parts[0].shape
    for at, ref in enumerate(parts):
        out_ref[:, at * n:(at + 1) * n, :] = jnp.swapaxes(ref[...], 0, 1)
    steps = jnp.concatenate([steps_ref[...].astype(F32), jnp.zeros((128 - n, heads), F32)], axis=0)
    last = len(parts) * n
    out_ref[:, last:last + 1, :] = jnp.transpose(steps).reshape(heads, 1, 128).astype(BF16)


def own_stats_kernel(n, scale, level_ref, own_ref, local_ref, max_ref, sum_ref):
    rows = max_ref.shape[0]
    heads = own_ref.shape[0]
    k, q = take(own_ref, 0, n), take(own_ref, 1, n)
    for at in range(0, rows, TILE):
        ti = slice(at, at + TILE)
        s = dot_nt(q[ti, :], k[0:at + TILE, :]) * scale
        row = lax.broadcasted_iota(jnp.int32, s.shape, 0) + at
        col = lax.broadcasted_iota(jnp.int32, s.shape, 1)
        add_stats(jnp.where(col <= row, s, LOWEST), max_ref, sum_ref, ti, True)

    level = jnp.full((1, 1), level_ref[0], jnp.int32).astype(F32)
    steps = own_ref[:, 4 * n:4 * n + 1, :].astype(F32).reshape(heads, 128)
    local = sums_rows(-jnp.exp2(-0.5 * level) * steps, rows, n)
    local_ref[...] = jnp.broadcast_to(local, local_ref.shape)


def stats_kernel(
    n, scale, block_ref, own_ref, in1_ref, in2_ref, in3_ref, local_ref, max_ref, sum_ref,
    out_ref, score_ref, q_s, k_s, max_s, sum_s,
):
    block = block_ref[0]
    k_s[0, :, :] = take(own_ref, 0, n)
    rows = q_s.shape[0]
    q_s[...] = take(own_ref, 1, n)
    max_s[...] = max_ref[...]
    sum_s[...] = sum_ref[...]
    for d, in_ref in enumerate((in1_ref, in2_ref, in3_ref)):
        k_s[d + 1, :, :] = take(in_ref, 0, n)

    @pl.loop(1, block + 1)
    def _(d):
        s = dot_nt(q_s[...], k_s[d]) * scale
        score_ref[d - 1, :, :] = s
        add_stats(s, max_s, sum_s, slice(None), False)

    @pl.loop(block + 1, 4)
    def _(d):
        score_ref[d - 1, :, :] = dot_nt(k_s[d], k_s[0]) * scale

    top = jnp.max(max_s[...], axis=1, keepdims=True)
    total = jnp.sum(sum_s[...] * jnp.exp2(max_s[...] - top), axis=1, keepdims=True)
    out_ref[...] = jnp.transpose(jnp.broadcast_to(top + jnp.log2(total), (rows, 8)))
    out_ref[2:3, :] = local_ref[0:1, :]


def fill_vec(block, stats_refs, vec_ref):
    local = [x[2:3, :] for x in stats_refs]
    rows = vec_ref.shape[1]
    ends = [x[:, rows - 1:rows] for x in local]
    vec_ref[0:1, :] = local[0]
    vec_ref[7:8, :] = jnp.zeros((1, rows), F32)
    for d in range(1, 4):
        nearer, farther = jnp.zeros((1, 1), F32), jnp.zeros((1, 1), F32)
        for g in range(1, d):
            nearer = nearer + ends[g]
        for g in range(d + 1, 4):
            farther = farther + ends[g]
        row_side = block >= d
        v = jnp.where(row_side, ends[d] - local[d], ends[0] - local[0])
        u = jnp.where(row_side, local[0] + nearer, local[d] + farther)
        vec_ref[d:d + 1, :] = jnp.exp2(v * LOG2E)
        vec_ref[3 + d:4 + d, :] = jnp.exp2(u * LOG2E)


def own_kernel(
    n, scale, beta, own_ref, stats_ref, gc_ref, gb_ref, sq_ref, gbt_s, cols_s,
):
    rows = gc_ref.shape[0]
    k_all, q_all, b_all, c_all = (take(own_ref, at, n) for at in range(4))
    ct = jnp.transpose(c_all.astype(F32)).astype(BF16)
    cols_s[...] = jnp.transpose(stats_ref[...])
    sq = jnp.zeros((8, 128), F32)
    gbt_s[...] = jnp.zeros(gbt_s.shape, F32)
    for i in range(0, rows, OWN):
        ti = slice(i, i + OWN)
        q, c = q_all[ti, :], c_all[ti, :]
        top_i, sum_i = cols_s[ti, 0:1], cols_s[ti, 2:3]
        gc = 0.0
        for j in range(0, i + OWN, OWN):
            tj = slice(j, j + OWN)
            k, b = k_all[tj, :], b_all[tj, :]
            s = dot_nt(q, k) * scale - top_i
            gap = sum_i - stats_ref[2:3, tj]
            if i == j:
                row = lax.broadcasted_iota(jnp.int32, s.shape, 0)
                col = lax.broadcasted_iota(jnp.int32, s.shape, 1)
                s = jnp.where(col <= row, s, LOWEST)
                gap = jnp.where(col <= row, gap, LOWEST)
            teacher = jnp.exp2(s)
            decay = jnp.exp2(gap * LOG2E)
            error = (dot_nt(c, b) * beta) * decay - teacher
            sq = sq + fold_rows(error * error)
            held = (error * decay).astype(BF16)
            gc = gc + dot_nn(held, b)
            gbt_s[:, tj] += dot_nn(ct[:, ti], held)
        gc_ref[ti, :] = gc
    gb_ref[...] = jnp.transpose(gbt_s[...])
    sq_ref[...] = sq


def blocks_kernel(
    n, beta, block_ref, own_ref, in1_ref, in2_ref, in3_ref, score_ref,
    stats_ref, st1_ref, st2_ref, st3_ref, gc_in_ref, gb_in_ref, sq_in_ref,
    gc_ref, gb_ref, out_ref,
    b_s, c_s, in_s, vec_s, cols_s, gbt_s, sq_s, cross_s,
):
    block = block_ref[0]
    rows, width = c_s.shape
    b_s[...] = take(own_ref, 2, n)
    c_s[...] = take(own_ref, 3, n)
    fill_vec(block, (stats_ref, st1_ref, st2_ref, st3_ref), vec_s)
    place = lax.broadcasted_iota(jnp.int32, (8, rows), 0)
    incoming = ((in1_ref, st1_ref), (in2_ref, st2_ref), (in3_ref, st3_ref))
    for d, (in_ref, st_ref) in enumerate(incoming, 1):
        in_s[d, :, :] = take(in_ref, 0, n)
        top = jnp.where(block >= d, stats_ref[0:1, :], st_ref[0:1, :])
        cols_s[d, :, :] = jnp.transpose(jnp.where(place == 0, top, vec_s[3 + d:4 + d, :]))
    gc_ref[...] = gc_in_ref[...]
    sq_s[...] = sq_in_ref[...]
    cross_s[...] = jnp.zeros(cross_s.shape, F32)
    gbt_s[...] = jnp.zeros(gbt_s.shape, F32)
    lane = lax.broadcasted_iota(jnp.int32, (1, 128), 1)

    @pl.loop(1, block + 1)
    def _(d):
        cross = jnp.zeros((1, 1), F32)
        sq = sq_s[...]
        for i in range(0, rows, TALL):
            ti = slice(i, i + TALL)
            held = []
            for j in range(0, rows, TILE):
                tj = slice(j, j + TILE)
                teacher = jnp.exp2(score_ref[d - 1, ti, tj] - cols_s[d, ti, 0:1])
                decay = cols_s[d, ti, 1:2] * vec_s[pl.ds(d, 1), tj]
                error = (dot_nt(c_s[ti, :], in_s[d, tj, :]) * beta) * decay - teacher
                sq = sq + fold_rows(error * error)
                held.append((error * decay).astype(BF16))
            gc = dot_nn(jnp.concatenate(held, axis=1), in_s[d])
            cross = cross + total_of(gc * c_s[ti, :].astype(F32))
            gc_ref[ti, :] += gc
        cross_s[...] += jnp.where((lane < block) & (lane >= block - d), cross * beta, 0.0)
        sq_s[...] = sq

    @pl.loop(block + 1, 4)
    def _(d):
        c = in_s[d]
        ct = jnp.transpose(c.astype(F32)).astype(BF16)
        top_i, u_i = cols_s[d, :, 0:1], cols_s[d, :, 1:2]
        for j in range(0, rows, WIDE):
            tj = slice(j, j + WIDE)
            teacher = jnp.exp2(score_ref[d - 1, :, tj] - top_i)
            decay = u_i * vec_s[pl.ds(d, 1), tj]
            error = (dot_nt(c, b_s[tj, :]) * beta) * decay - teacher
            gbt_s[:, tj] += dot_nn(ct, (error * decay).astype(BF16))

    gb_ref[...] = gb_in_ref[...] + jnp.transpose(gbt_s[...])
    sums = jnp.where(lane == 3, total_of(sq_s[...]), cross_s[...])
    out_ref[...] = jnp.broadcast_to(sums, out_ref.shape)


def prepare_kernel(n, beta, own_ref, gc_ref, gb_ref, out_ref, tail_ref, exp_ref):
    heads, _, width = own_ref.shape
    rows = heads * n
    gb = gb_ref[...]
    gc = gc_ref[...]
    c = take(own_ref, 3, n).astype(F32)
    b = take(own_ref, 2, n).astype(F32)
    slope = jnp.sum(c * gc - b * gb, axis=1, keepdims=True) * beta
    slope = jnp.broadcast_to(slope, (rows, 128)).reshape(heads, n, 128)
    place = lax.broadcasted_iota(jnp.int32, (heads, n, 128), 1)
    lane3 = lax.broadcasted_iota(jnp.int32, (heads, n, 128), 2)
    slope = jnp.sum(jnp.where(place == lane3 % n, slope, 0.0), axis=1)
    up = lax.broadcasted_iota(jnp.int32, (128, 128), 0)
    across = lax.broadcasted_iota(jnp.int32, (128, 128), 1)
    same = up // n == across // n
    inside = dot_full(slope, jnp.where(same & (up >= across), 1.0, 0.0).astype(F32))
    whole = dot_full(slope, jnp.where(same, 1.0, 0.0).astype(F32))
    down = lax.broadcasted_iota(jnp.int32, (heads, heads), 0)
    right = lax.broadcasted_iota(jnp.int32, (heads, heads), 1)
    behind = dot_full(jnp.where(right > down, 1.0, 0.0).astype(F32), whole)
    tail_ref[...] = inside + behind
    eb, ec = exponent_of(gb), exponent_of(gc)
    out_ref[:, 0:n, :] = (gb * jnp.exp2(14.0 - eb)).reshape(heads, n, width)
    out_ref[:, n:2 * n, :] = (gc * jnp.exp2(14.0 - ec)).reshape(heads, n, width)
    place = lax.broadcasted_iota(jnp.int32, exp_ref.shape, 0)
    exp_ref[...] = jnp.where(place == 0, eb, ec)


def finish_kernel(
    n, seq_len, block_ref, level_ref, grads_ref, tail_ref, exp_ref,
    sums0_ref, sums1_ref, sums2_ref, sums3_ref, out_ref,
):
    block = block_ref[0]
    heads = out_ref.shape[0]
    out_ref[:, 0:2 * n, :] = grads_ref[...]
    lane1 = lax.broadcasted_iota(jnp.int32, (1, 128), 1)
    sums = (sums0_ref[0:1, :] + sums1_ref[0:1, :]) + (sums2_ref[0:1, :] + sums3_ref[0:1, :])
    after = jnp.sum(
        jnp.where(jnp.logical_and(lane1 == block, block < 3), sums, 0.0), axis=1, keepdims=True
    )
    error_sq = jnp.sum(jnp.where(lane1 == 3, sums, 0.0), axis=1, keepdims=True)
    norm = jnp.sqrt(error_sq + 1e-06)
    factor = seq_len / norm
    rate = jnp.exp2(-0.5 * jnp.full((1, 1), level_ref[0], jnp.int32).astype(F32))
    step = (tail_ref[...] + after) * (-(rate * factor))
    lane = lax.broadcasted_iota(jnp.int32, (heads, 128), 1)
    eb, ec = exp_ref[0:1, 0:1], exp_ref[1:2, 0:1]
    es, en = exponent_of(step), exponent_of(norm)
    high, low = split_scaled(step, es)
    norm_high, norm_low = split_scaled(norm, en)
    last = jnp.where(lane < n, high, low)
    for at, value in enumerate((eb, ec, es, norm_high, norm_low, en)):
        last = jnp.where(lane == 2 * n + at, value, last)
    out_ref[:, 2 * n:2 * n + 1, :] = last.reshape(heads, 1, 128)


def unpack_kernel(beta, seq_len, x_ref, gb_ref, gc_ref, step_ref, loss_ref):
    heads = x_ref.shape[0]
    n = gb_ref.shape[0]
    last = x_ref[:, 2 * n:2 * n + 1, :].reshape(heads, 128)
    lane = lax.broadcasted_iota(jnp.int32, (heads, 128), 1)

    def pick(at):
        return jnp.sum(jnp.where(lane == 2 * n + at, last, 0.0), axis=1, keepdims=True)

    scale_b, scale_c, scale_s = (jnp.exp2(pick(at) - 14.0) for at in range(3))
    norm = (pick(3) + pick(4)) * jnp.exp2(pick(5) - 14.0)
    scale_b, scale_c = (x * (seq_len / norm * beta) for x in (scale_b, scale_c))
    gb_ref[...] = jnp.swapaxes(x_ref[:, 0:n, :] * scale_b[:, :, None], 0, 1)
    gc_ref[...] = jnp.swapaxes(x_ref[:, n:2 * n, :] * scale_c[:, :, None], 0, 1)
    step = jnp.transpose(last * scale_s)
    step_ref[...] = step[0:n, :] + step[n:2 * n, :]
    loss_ref[...] = jnp.sum(norm, axis=0, keepdims=True) * (1.0 / heads)


def call(kernel, out_shape, scratch, scalars, count):
    return pl.pallas_call(
        kernel,
        out_shape=out_shape,
        in_specs=[pl.BlockSpec(memory_space=pltpu.SMEM)] * scalars
        + [pl.BlockSpec(memory_space=pltpu.VMEM)] * (count - scalars),
        out_specs=jax.tree.map(lambda _: pl.BlockSpec(memory_space=pltpu.VMEM), out_shape),
        scratch_shapes=scratch,
        compiler_params=pltpu.CompilerParams(vmem_limit_bytes=VMEM_BYTES),
    )


def shape(*dims, dtype=F32):
    return jax.ShapeDtypeStruct(dims, dtype)


def near(*dims, dtype=F32):
    return pltpu.VMEM(dims, dtype)


def held_near(x):
    return pltpu.with_memory_space_constraint(x, pltpu.VMEM)


def per_device(queries, keys, b_proj, c_proj, step_size, rate_level):
    n, heads, width = queries.shape
    blocks = lax.axis_size("seq")
    block = lax.axis_index("seq")
    rows = n * heads
    seq_len = rows * blocks
    beta = 2.0 / math.sqrt(width * seq_len)
    scale = LOG2E / math.sqrt(width)

    def to_heads(x):
        return lax.all_to_all(x, "head", split_axis=0, concat_axis=0, tiled=True)

    def around(x):
        return [
            lax.ppermute(x, "seq", [(i, (i + d) % blocks) for i in range(blocks)])
            for d in range(1, blocks)
        ]

    def exchange(pair, ahead=None):
        mine, after = pair[:, 0:n], pair[:, n:2 * n]
        out = []
        for d in range(1, blocks):
            sent = jnp.where(block + d < blocks, mine, after)
            if ahead is not None and d == 1:
                sent, ahead[2] = lax.optimization_barrier((sent, ahead[2]))
            out.append(
                lax.ppermute(sent, "seq", [(i, (i + d) % blocks) for i in range(blocks)])
            )
        return out

    inputs = [
        pltpu.with_memory_space_constraint(x, pltpu.HBM)
        for x in (keys, queries, b_proj, c_proj, step_size)
    ]
    arrived = to_heads(
        call(pack_kernel, near(heads, 4 * n + 1, width, dtype=BF16), [], 0, 5)(*inputs)
    )
    kq_from = exchange(arrived[:, 0:2 * n])
    own = held_near(arrived)
    where = jnp.reshape(block, (1,)).astype(jnp.int32)
    mat = pltpu.VMEM((rows, width), BF16)
    mats = pltpu.VMEM((blocks, rows, width), BF16)
    flat = pltpu.VMEM((width, rows), F32)
    state = pltpu.VMEM((rows, 128), F32)
    local, top, total = call(
        functools.partial(own_stats_kernel, n, scale),
        [near(8, rows), near(rows, 128), near(rows, 128)], [], 1, 2,
    )(rate_level, own)
    bc, local = lax.optimization_barrier((arrived[:, 2 * n:4 * n], local))
    bc_from = exchange(bc, kq_from)
    kq_from, bc_from = [[held_near(x) for x in y] for y in (kq_from, bc_from)]
    stats, scores = call(
        functools.partial(stats_kernel, n, scale),
        [near(8, rows), near(blocks - 1, rows, rows)], [mat, mats, state, state], 1, 8,
    )(where, own, *kq_from, local, top, total)
    stats_from = [held_near(x) for x in around(stats)]
    gc, gb, sq = call(
        functools.partial(own_kernel, n, scale, beta),
        [near(rows, width), near(rows, width), near(8, 128)],
        [flat, pltpu.VMEM((rows, 8), F32)], 0, 2,
    )(own, stats)
    gc, gb, sums = call(
        functools.partial(blocks_kernel, n, beta),
        [near(rows, width), near(rows, width), near(8, 128)],
        [
            mat, mat, mats, pltpu.VMEM((8, rows), F32), pltpu.VMEM((4, rows, 8), F32), flat,
            pltpu.VMEM((8, 128), F32), pltpu.VMEM((1, 128), F32),
        ],
        1, 13,
    )(where, own, *bc_from, scores, stats, *stats_from, gc, gb, sq)
    sums_from = [held_near(x) for x in around(sums)]
    packed, tail, exps = call(
        functools.partial(prepare_kernel, n, beta),
        [near(heads, 2 * n, width), near(heads, 128), near(8, 128)], [], 0, 3,
    )(own, gc, gb)
    packed = call(
        functools.partial(finish_kernel, n, float(seq_len)),
        near(heads, 2 * n + 1, width), [], 2, 9,
    )(where, rate_level, packed, tail, exps, sums, *sums_from)
    back = to_heads(packed.astype(F16)).astype(F32)
    grad_b, grad_c, grad_step, loss = pl.pallas_call(
        functools.partial(unpack_kernel, beta, float(seq_len)),
        out_shape=[
            shape(n, heads, width), shape(n, heads, width), shape(n, heads), shape(1, 1),
        ],
        compiler_params=pltpu.CompilerParams(vmem_limit_bytes=VMEM_BYTES),
    )(held_near(back))
    return grad_b, grad_c, grad_step, jnp.reshape(loss, ())


def solution(mesh):
    tokens = P(("seq", "head"), None, None)
    return jax.shard_map(
        per_device,
        mesh=mesh,
        in_specs=(tokens, tokens, tokens, tokens, P(("seq", "head"), None), P("head")),
        out_specs=(tokens, tokens, P(("seq", "head"), None), P()),
        check_vma=False,
    )
```

```python
import functools
import math

import jax
import jax.numpy as jnp
from jax import lax
from jax.experimental import pallas as pl
from jax.experimental.pallas import tpu as pltpu
from jax.sharding import PartitionSpec as P

F32 = jnp.float32
BF16 = jnp.bfloat16
F16 = jnp.float16
LOG2E = math.log2(math.e)
TILE = 256
TALL = 512
WIDE = 1024
OWN = 512
LOWEST = -1e30
VMEM_BYTES = 32 * 1024 * 1024


def dot_nt(a, b):
    return lax.dot_general(a, b, (((1,), (1,)), ((), ())), preferred_element_type=F32)


def dot_nn(a, b):
    return lax.dot_general(a, b, (((1,), (0,)), ((), ())), preferred_element_type=F32)


def dot_full(a, b):
    return lax.dot_general(
        a, b, (((1,), (0,)), ((), ())),
        precision=lax.Precision.HIGHEST, preferred_element_type=F32,
    )


def fold_rows(x):
    rows, cols = x.shape
    x = jnp.sum(x.reshape(rows // 8, 8, cols), axis=0)
    out = x[:, :128]
    for at in range(128, cols, 128):
        out = out + x[:, at:at + 128]
    return out


def total_of(x):
    return jnp.sum(jnp.sum(x, axis=0, keepdims=True), axis=1, keepdims=True)


def exponent_of(x):
    top = jnp.max(jnp.max(jnp.abs(x), axis=0, keepdims=True), axis=1, keepdims=True)
    return jnp.floor(jnp.log2(jnp.maximum(top, 1e-30)))


def sums_rows(log_decay, rows, n):
    heads, lanes = log_decay.shape
    up = lax.broadcasted_iota(jnp.int32, (lanes, lanes), 0)
    across = lax.broadcasted_iota(jnp.int32, (lanes, lanes), 1)
    same = up // n == across // n
    inside = dot_full(log_decay, jnp.where(same & (up <= across), 1.0, 0.0).astype(F32))
    whole = dot_full(log_decay, jnp.where(same, 1.0, 0.0).astype(F32))
    down = lax.broadcasted_iota(jnp.int32, (heads, heads), 0)
    right = lax.broadcasted_iota(jnp.int32, (heads, heads), 1)
    sums = inside + dot_full(jnp.where(right < down, 1.0, 0.0).astype(F32), whole)
    lane = lax.broadcasted_iota(jnp.int32, (lanes, rows), 0)
    place = lax.broadcasted_iota(jnp.int32, (lanes, rows), 1)
    owner = lax.broadcasted_iota(jnp.int32, (heads, rows), 0)
    token = lax.broadcasted_iota(jnp.int32, (heads, rows), 1)
    high = sums.astype(BF16)
    rest = sums - high.astype(F32)
    mid = rest.astype(BF16)
    low = (rest - mid.astype(F32)).astype(BF16)
    terms = jnp.concatenate([high, mid, low], axis=0)
    pick = jnp.where(lane == place % n, 1.0, 0.0).astype(BF16)
    spread = dot_nn(terms, pick)
    spread = spread[0:heads] + spread[heads:2 * heads] + spread[2 * heads:]
    return jnp.sum(jnp.where(token // n == owner, spread, 0.0), axis=0, keepdims=True)


def split_scaled(x, e):
    y = x * jnp.exp2(14.0 - e)
    high = jnp.floor(y * (1.0 / 16.0)) * 16.0
    return high, y - high


def add_stats(s, max_ref, sum_ref, ti, first):
    new = LOWEST if first else max_ref[ti, :]
    size = s.shape[1]
    for g in range(0, size, 128):
        new = jnp.maximum(new, s[:, g:g + 128])
    acc = 0.0 if first else sum_ref[ti, :] * jnp.exp2(max_ref[ti, :] - new)
    for g in range(0, size, 128):
        acc = acc + jnp.exp2(s[:, g:g + 128] - new)
    max_ref[ti, :] = new
    sum_ref[ti, :] = acc


def take(ref, at, n):
    heads, _, width = ref.shape
    return ref[:, at * n:(at + 1) * n, :].reshape(heads * n, width)


def pack_kernel(*refs):
    parts, steps_ref, out_ref = refs[:-2], refs[-2], refs[-1]
    n, heads, _ = parts[0].shape
    for at, ref in enumerate(parts):
        out_ref[:, at * n:(at + 1) * n, :] = jnp.swapaxes(ref[...], 0, 1)
    steps = jnp.concatenate([steps_ref[...].astype(F32), jnp.zeros((128 - n, heads), F32)], axis=0)
    last = len(parts) * n
    out_ref[:, last:last + 1, :] = jnp.transpose(steps).reshape(heads, 1, 128).astype(BF16)


def own_stats_kernel(n, scale, level_ref, own_ref, local_ref, max_ref, sum_ref):
    rows = max_ref.shape[0]
    heads = own_ref.shape[0]
    k, q = take(own_ref, 0, n), take(own_ref, 1, n)
    for at in range(0, rows, TILE):
        ti = slice(at, at + TILE)
        s = dot_nt(q[ti, :], k[0:at + TILE, :]) * scale
        row = lax.broadcasted_iota(jnp.int32, s.shape, 0) + at
        col = lax.broadcasted_iota(jnp.int32, s.shape, 1)
        add_stats(jnp.where(col <= row, s, LOWEST), max_ref, sum_ref, ti, True)

    level = jnp.full((1, 1), level_ref[0], jnp.int32).astype(F32)
    steps = own_ref[:, 4 * n:4 * n + 1, :].astype(F32).reshape(heads, 128)
    local = sums_rows(-jnp.exp2(-0.5 * level) * steps, rows, n)
    local_ref[...] = jnp.broadcast_to(local, local_ref.shape)


def stats_kernel(
    n, scale, block_ref, own_ref, in1_ref, in2_ref, in3_ref, local_ref, max_ref, sum_ref,
    out_ref, score_ref, q_s, k_s, max_s, sum_s,
):
    block = block_ref[0]
    k_s[0, :, :] = take(own_ref, 0, n)
    rows = q_s.shape[0]
    q_s[...] = take(own_ref, 1, n)
    max_s[...] = max_ref[...]
    sum_s[...] = sum_ref[...]
    for d, in_ref in enumerate((in1_ref, in2_ref, in3_ref)):
        k_s[d + 1, :, :] = take(in_ref, 0, n)

    @pl.loop(1, block + 1)
    def _(d):
        for at in range(0, q_s.shape[0], TALL):
            ti = slice(at, at + TALL)
            s = dot_nt(q_s[ti, :], k_s[d]) * scale
            score_ref[d - 1, ti, :] = s
            add_stats(s, max_s, sum_s, ti, False)

    @pl.loop(block + 1, 4)
    def _(d):
        score_ref[d - 1, :, :] = dot_nt(k_s[d], k_s[0]) * scale

    top = jnp.max(max_s[...], axis=1, keepdims=True)
    total = jnp.sum(sum_s[...] * jnp.exp2(max_s[...] - top), axis=1, keepdims=True)
    out_ref[...] = jnp.transpose(jnp.broadcast_to(top + jnp.log2(total), (rows, 8)))
    out_ref[2:3, :] = local_ref[0:1, :]


def fill_vec(block, stats_refs, vec_ref):
    local = [x[2:3, :] for x in stats_refs]
    rows = vec_ref.shape[1]
    ends = [x[:, rows - 1:rows] for x in local]
    vec_ref[0:1, :] = local[0]
    vec_ref[7:8, :] = jnp.zeros((1, rows), F32)
    for d in range(1, 4):
        nearer, farther = jnp.zeros((1, 1), F32), jnp.zeros((1, 1), F32)
        for g in range(1, d):
            nearer = nearer + ends[g]
        for g in range(d + 1, 4):
            farther = farther + ends[g]
        row_side = block >= d
        v = jnp.where(row_side, ends[d] - local[d], ends[0] - local[0])
        u = jnp.where(row_side, local[0] + nearer, local[d] + farther)
        vec_ref[d:d + 1, :] = jnp.exp2(v * LOG2E)
        vec_ref[3 + d:4 + d, :] = jnp.exp2(u * LOG2E)


def own_kernel(
    n, scale, beta, own_ref, stats_ref, gc_ref, gb_ref, sq_ref, gbt_s, cols_s,
):
    rows = gc_ref.shape[0]
    k_all, q_all, b_all, c_all = (take(own_ref, at, n) for at in range(4))
    ct = jnp.transpose(c_all.astype(F32)).astype(BF16)
    cols_s[...] = jnp.transpose(stats_ref[...])
    sq = jnp.zeros((8, 128), F32)
    gbt_s[...] = jnp.zeros(gbt_s.shape, F32)
    for i in range(0, rows, OWN):
        ti = slice(i, i + OWN)
        q, c = q_all[ti, :], c_all[ti, :]
        top_i, sum_i = cols_s[ti, 0:1], cols_s[ti, 2:3]
        gc = 0.0
        for j in range(0, i + OWN, OWN):
            tj = slice(j, j + OWN)
            k, b = k_all[tj, :], b_all[tj, :]
            s = dot_nt(q, k) * scale - top_i
            gap = sum_i - stats_ref[2:3, tj]
            if i == j:
                row = lax.broadcasted_iota(jnp.int32, s.shape, 0)
                col = lax.broadcasted_iota(jnp.int32, s.shape, 1)
                s = jnp.where(col <= row, s, LOWEST)
                gap = jnp.where(col <= row, gap, LOWEST)
            teacher = jnp.exp2(s)
            decay = jnp.exp2(gap * LOG2E)
            error = (dot_nt(c, b) * beta) * decay - teacher
            sq = sq + fold_rows(error * error)
            held = (error * decay).astype(BF16)
            gc = gc + dot_nn(held, b)
            gbt_s[:, tj] += dot_nn(ct[:, ti], held)
        gc_ref[ti, :] = gc
    gb_ref[...] = jnp.transpose(gbt_s[...])
    sq_ref[...] = sq


def blocks_kernel(
    n, beta, block_ref, own_ref, in1_ref, in2_ref, in3_ref, score_ref,
    stats_ref, st1_ref, st2_ref, st3_ref, gc_in_ref, gb_in_ref, sq_in_ref,
    gc_ref, gb_ref, out_ref,
    b_s, c_s, in_s, vec_s, cols_s, gbt_s, sq_s, cross_s,
):
    block = block_ref[0]
    rows, width = c_s.shape
    b_s[...] = take(own_ref, 2, n)
    c_s[...] = take(own_ref, 3, n)
    fill_vec(block, (stats_ref, st1_ref, st2_ref, st3_ref), vec_s)
    place = lax.broadcasted_iota(jnp.int32, (8, rows), 0)
    incoming = ((in1_ref, st1_ref), (in2_ref, st2_ref), (in3_ref, st3_ref))
    for d, (in_ref, st_ref) in enumerate(incoming, 1):
        in_s[d, :, :] = take(in_ref, 0, n)
        top = jnp.where(block >= d, stats_ref[0:1, :], st_ref[0:1, :])
        cols_s[d, :, :] = jnp.transpose(jnp.where(place == 0, top, vec_s[3 + d:4 + d, :]))
    gc_ref[...] = gc_in_ref[...]
    sq_s[...] = sq_in_ref[...]
    cross_s[...] = jnp.zeros(cross_s.shape, F32)
    gbt_s[...] = jnp.zeros(gbt_s.shape, F32)
    lane = lax.broadcasted_iota(jnp.int32, (1, 128), 1)

    @pl.loop(1, block + 1)
    def _(d):
        cross = jnp.zeros((1, 1), F32)
        sq = sq_s[...]
        for i in range(0, rows, TALL):
            ti = slice(i, i + TALL)
            held = []
            for j in range(0, rows, TILE):
                tj = slice(j, j + TILE)
                teacher = jnp.exp2(score_ref[d - 1, ti, tj] - cols_s[d, ti, 0:1])
                decay = cols_s[d, ti, 1:2] * vec_s[pl.ds(d, 1), tj]
                error = (dot_nt(c_s[ti, :], in_s[d, tj, :]) * beta) * decay - teacher
                sq = sq + fold_rows(error * error)
                held.append((error * decay).astype(BF16))
            gc = dot_nn(jnp.concatenate(held, axis=1), in_s[d])
            cross = cross + total_of(gc * c_s[ti, :].astype(F32))
            gc_ref[ti, :] += gc
        cross_s[...] += jnp.where((lane < block) & (lane >= block - d), cross * beta, 0.0)
        sq_s[...] = sq

    @pl.loop(block + 1, 4)
    def _(d):
        c = in_s[d]
        ct = jnp.transpose(c.astype(F32)).astype(BF16)
        top_i, u_i = cols_s[d, :, 0:1], cols_s[d, :, 1:2]
        for j in range(0, rows, WIDE):
            tj = slice(j, j + WIDE)
            teacher = jnp.exp2(score_ref[d - 1, :, tj] - top_i)
            decay = u_i * vec_s[pl.ds(d, 1), tj]
            error = (dot_nt(c, b_s[tj, :]) * beta) * decay - teacher
            gbt_s[:, tj] += dot_nn(ct, (error * decay).astype(BF16))

    gb_ref[...] = gb_in_ref[...] + jnp.transpose(gbt_s[...])
    sums = jnp.where(lane == 3, total_of(sq_s[...]), cross_s[...])
    out_ref[...] = jnp.broadcast_to(sums, out_ref.shape)


def prepare_kernel(n, beta, own_ref, gc_ref, gb_ref, out_ref, tail_ref, exp_ref):
    heads, _, width = own_ref.shape
    rows = heads * n
    gb = gb_ref[...]
    gc = gc_ref[...]
    c = take(own_ref, 3, n).astype(F32)
    b = take(own_ref, 2, n).astype(F32)
    slope = jnp.sum(c * gc - b * gb, axis=1, keepdims=True) * beta
    slope = jnp.broadcast_to(slope, (rows, 128)).reshape(heads, n, 128)
    place = lax.broadcasted_iota(jnp.int32, (heads, n, 128), 1)
    lane3 = lax.broadcasted_iota(jnp.int32, (heads, n, 128), 2)
    slope = jnp.sum(jnp.where(place == lane3 % n, slope, 0.0), axis=1)
    up = lax.broadcasted_iota(jnp.int32, (128, 128), 0)
    across = lax.broadcasted_iota(jnp.int32, (128, 128), 1)
    same = up // n == across // n
    inside = dot_full(slope, jnp.where(same & (up >= across), 1.0, 0.0).astype(F32))
    whole = dot_full(slope, jnp.where(same, 1.0, 0.0).astype(F32))
    down = lax.broadcasted_iota(jnp.int32, (heads, heads), 0)
    right = lax.broadcasted_iota(jnp.int32, (heads, heads), 1)
    behind = dot_full(jnp.where(right > down, 1.0, 0.0).astype(F32), whole)
    tail_ref[...] = inside + behind
    eb, ec = exponent_of(gb), exponent_of(gc)
    out_ref[:, 0:n, :] = (gb * jnp.exp2(14.0 - eb)).reshape(heads, n, width)
    out_ref[:, n:2 * n, :] = (gc * jnp.exp2(14.0 - ec)).reshape(heads, n, width)
    place = lax.broadcasted_iota(jnp.int32, exp_ref.shape, 0)
    exp_ref[...] = jnp.where(place == 0, eb, ec)


def finish_kernel(
    n, seq_len, block_ref, level_ref, grads_ref, tail_ref, exp_ref,
    sums0_ref, sums1_ref, sums2_ref, sums3_ref, out_ref,
):
    block = block_ref[0]
    heads = out_ref.shape[0]
    out_ref[:, 0:2 * n, :] = grads_ref[...]
    lane1 = lax.broadcasted_iota(jnp.int32, (1, 128), 1)
    sums = (sums0_ref[0:1, :] + sums1_ref[0:1, :]) + (sums2_ref[0:1, :] + sums3_ref[0:1, :])
    after = jnp.sum(
        jnp.where(jnp.logical_and(lane1 == block, block < 3), sums, 0.0), axis=1, keepdims=True
    )
    error_sq = jnp.sum(jnp.where(lane1 == 3, sums, 0.0), axis=1, keepdims=True)
    norm = jnp.sqrt(error_sq + 1e-06)
    factor = seq_len / norm
    rate = jnp.exp2(-0.5 * jnp.full((1, 1), level_ref[0], jnp.int32).astype(F32))
    step = (tail_ref[...] + after) * (-(rate * factor))
    lane = lax.broadcasted_iota(jnp.int32, (heads, 128), 1)
    eb, ec = exp_ref[0:1, 0:1], exp_ref[1:2, 0:1]
    es, en = exponent_of(step), exponent_of(norm)
    high, low = split_scaled(step, es)
    norm_high, norm_low = split_scaled(norm, en)
    last = jnp.where(lane < n, high, low)
    for at, value in enumerate((eb, ec, es, norm_high, norm_low, en)):
        last = jnp.where(lane == 2 * n + at, value, last)
    out_ref[:, 2 * n:2 * n + 1, :] = last.reshape(heads, 1, 128)


def unpack_kernel(beta, seq_len, x_ref, gb_ref, gc_ref, step_ref, loss_ref):
    heads = x_ref.shape[0]
    n = gb_ref.shape[0]
    last = x_ref[:, 2 * n:2 * n + 1, :].reshape(heads, 128)
    lane = lax.broadcasted_iota(jnp.int32, (heads, 128), 1)

    def pick(at):
        return jnp.sum(jnp.where(lane == 2 * n + at, last, 0.0), axis=1, keepdims=True)

    scale_b, scale_c, scale_s = (jnp.exp2(pick(at) - 14.0) for at in range(3))
    norm = (pick(3) + pick(4)) * jnp.exp2(pick(5) - 14.0)
    scale_b, scale_c = (x * (seq_len / norm * beta) for x in (scale_b, scale_c))
    gb_ref[...] = jnp.swapaxes(x_ref[:, 0:n, :] * scale_b[:, :, None], 0, 1)
    gc_ref[...] = jnp.swapaxes(x_ref[:, n:2 * n, :] * scale_c[:, :, None], 0, 1)
    step = jnp.transpose(last * scale_s)
    step_ref[...] = step[0:n, :] + step[n:2 * n, :]
    loss_ref[...] = jnp.sum(norm, axis=0, keepdims=True) * (1.0 / heads)


def call(kernel, out_shape, scratch, scalars, count):
    return pl.pallas_call(
        kernel,
        out_shape=out_shape,
        in_specs=[pl.BlockSpec(memory_space=pltpu.SMEM)] * scalars
        + [pl.BlockSpec(memory_space=pltpu.VMEM)] * (count - scalars),
        out_specs=jax.tree.map(lambda _: pl.BlockSpec(memory_space=pltpu.VMEM), out_shape),
        scratch_shapes=scratch,
        compiler_params=pltpu.CompilerParams(vmem_limit_bytes=VMEM_BYTES),
    )


def shape(*dims, dtype=F32):
    return jax.ShapeDtypeStruct(dims, dtype)


def near(*dims, dtype=F32):
    return pltpu.VMEM(dims, dtype)


def held_near(x):
    return pltpu.with_memory_space_constraint(x, pltpu.VMEM)


def per_device(queries, keys, b_proj, c_proj, step_size, rate_level):
    n, heads, width = queries.shape
    blocks = lax.axis_size("seq")
    block = lax.axis_index("seq")
    rows = n * heads
    seq_len = rows * blocks
    beta = 2.0 / math.sqrt(width * seq_len)
    scale = LOG2E / math.sqrt(width)

    def to_heads(x):
        return lax.all_to_all(x, "head", split_axis=0, concat_axis=0, tiled=True)

    def around(x):
        return [
            lax.ppermute(x, "seq", [(i, (i + d) % blocks) for i in range(blocks)])
            for d in range(1, blocks)
        ]

    def exchange(pair, ahead=None):
        mine, after = pair[:, 0:n], pair[:, n:2 * n]
        out = []
        for d in range(1, blocks):
            sent = jnp.where(block + d < blocks, mine, after)
            if ahead is not None and d == 1:
                sent, ahead[2] = lax.optimization_barrier((sent, ahead[2]))
            out.append(
                lax.ppermute(sent, "seq", [(i, (i + d) % blocks) for i in range(blocks)])
            )
        return out

    inputs = [
        pltpu.with_memory_space_constraint(x, pltpu.HBM)
        for x in (keys, queries, b_proj, c_proj, step_size)
    ]
    arrived = to_heads(
        call(pack_kernel, near(heads, 4 * n + 1, width, dtype=BF16), [], 0, 5)(*inputs)
    )
    kq_from = exchange(arrived[:, 0:2 * n])
    own = held_near(arrived)
    where = jnp.reshape(block, (1,)).astype(jnp.int32)
    mat = pltpu.VMEM((rows, width), BF16)
    mats = pltpu.VMEM((blocks, rows, width), BF16)
    flat = pltpu.VMEM((width, rows), F32)
    state = pltpu.VMEM((rows, 128), F32)
    local, top, total = call(
        functools.partial(own_stats_kernel, n, scale),
        [near(8, rows), near(rows, 128), near(rows, 128)], [], 1, 2,
    )(rate_level, own)
    bc, local = lax.optimization_barrier((arrived[:, 2 * n:4 * n], local))
    bc_from = exchange(bc, kq_from)
    kq_from, bc_from = [[held_near(x) for x in y] for y in (kq_from, bc_from)]
    stats, scores = call(
        functools.partial(stats_kernel, n, scale),
        [near(8, rows), near(blocks - 1, rows, rows)], [mat, mats, state, state], 1, 8,
    )(where, own, *kq_from, local, top, total)
    stats_from = [held_near(x) for x in around(stats)]
    gc, gb, sq = call(
        functools.partial(own_kernel, n, scale, beta),
        [near(rows, width), near(rows, width), near(8, 128)],
        [flat, pltpu.VMEM((rows, 8), F32)], 0, 2,
    )(own, stats)
    gc, gb, sums = call(
        functools.partial(blocks_kernel, n, beta),
        [near(rows, width), near(rows, width), near(8, 128)],
        [
            mat, mat, mats, pltpu.VMEM((8, rows), F32), pltpu.VMEM((4, rows, 8), F32), flat,
            pltpu.VMEM((8, 128), F32), pltpu.VMEM((1, 128), F32),
        ],
        1, 13,
    )(where, own, *bc_from, scores, stats, *stats_from, gc, gb, sq)
    sums_from = [held_near(x) for x in around(sums)]
    packed, tail, exps = call(
        functools.partial(prepare_kernel, n, beta),
        [near(heads, 2 * n, width), near(heads, 128), near(8, 128)], [], 0, 3,
    )(own, gc, gb)
    packed = call(
        functools.partial(finish_kernel, n, float(seq_len)),
        near(heads, 2 * n + 1, width), [], 2, 9,
    )(where, rate_level, packed, tail, exps, sums, *sums_from)
    back = to_heads(packed.astype(F16)).astype(F32)
    grad_b, grad_c, grad_step, loss = pl.pallas_call(
        functools.partial(unpack_kernel, beta, float(seq_len)),
        out_shape=[
            shape(n, heads, width), shape(n, heads, width), shape(n, heads), shape(1, 1),
        ],
        compiler_params=pltpu.CompilerParams(vmem_limit_bytes=VMEM_BYTES),
    )(held_near(back))
    return grad_b, grad_c, grad_step, jnp.reshape(loss, ())


def solution(mesh):
    tokens = P(("seq", "head"), None, None)
    return jax.shard_map(
        per_device,
        mesh=mesh,
        in_specs=(tokens, tokens, tokens, tokens, P(("seq", "head"), None), P("head")),
        out_specs=(tokens, tokens, P(("seq", "head"), None), P()),
        check_vma=False,
    )
```
